512 devices in a mesh: shot: 16 (over y_lo, x), space: 32 (over z, y_hi, core).
Axes of the slice: x: 4, y: 8 (y_hi: 2, y_lo: 4; y = y_hi * 4 + y_lo), z: 8, core: 2. Of those that a mesh axis runs over, the one named last changes fastest.
Arguments:
- courant: float32 [512, 256, 128], P('shot', 'space'), may hold values from 0.05 to 0.18
- anchor: int32 [16, 2], P('shot'), may hold values from 0 to 384, as said below
- source: int32 [16, 3], P('shot'), may hold values from 0 to 127, as said below
- wavelet: float32 [16, 3], P('shot'), may hold values from -12 to 12
- receivers: int32 [16, 64, 3], P('shot'), may hold values from 0 to 127, as said below
- observed: float32 [16, 3, 64], P('shot'), may hold values from -3 to 3
- wave_before: float32 [16, 128, 128, 128], P('shot', 'space'), may hold values from -1.8 to 1.8
- wave_now: float32 [16, 128, 128, 128], P('shot', 'space'), may hold values from -1.8 to 1.8
- adjoint_after: float32 [16, 128, 128, 128], P('shot', 'space'), may hold values from -1.8 to 1.8
- adjoint_now: float32 [16, 128, 128, 128], P('shot', 'space'), may hold values from -1.8 to 1.8
Outputs:
- gradient: float32 [512, 256, 128], P('shot', 'space')
The draws below stay inside these ranges and needn't reach their ends.
Inputs may be any that keep to these rules, and one draw needn't show every extreme that they name: anchor[s] = (ox, oy) with ox at most 384 and oy at most 128; in each column some shot group has 0 and some the column's largest allowed value. `source`: a cell of the aperture: first coordinate below 128, second below 128, third below 128; in each column some shot group has 0 and some the largest value. `receivers`: cells of the aperture: first coordinate below 128, second below 128, third below 128; cells may repeat; in each column some receiver has 0 and some the largest value.
All inputs are finite; a program needn't handle non-finite values.
Results may differ from the reference program's by a relative error of at most 0.00002.
Values sent between devices are 32-bit elements; how exact they have to be, the bound alone decides.
A program may use at most 64 MiB of HBM per device.

```python
import math
import jax
import jax.numpy as jnp
from jax import lax

MZ = 128
STEPS = 3
NREC = 64
SHOTS = 16
MX = 512
MY = 256
AX = 128
AY = 128


def forced_column(key, item_count, highest):
    values = jax.random.randint(key, (item_count,), 0, highest + 1)
    first_pick = jax.random.randint(jax.random.fold_in(key, 1), (), 0, item_count)
    second_pick = (first_pick + 1 + jax.random.randint(jax.random.fold_in(key, 2), (), 0, item_count - 1)) % item_count
    return values.at[first_pick].set(highest).at[second_pick].set(0)


def cell_rows(key, item_count):
    first = forced_column(jax.random.fold_in(key, 41), item_count, AX - 1)
    second = forced_column(jax.random.fold_in(key, 42), item_count, AY - 1)
    third = forced_column(jax.random.fold_in(key, 43), item_count, MZ - 1)
    return jnp.stack([first, second, third], axis=1).astype(jnp.int32)


def draw_anchor(key, part):
    first = forced_column(jax.random.fold_in(key, 11), SHOTS, MX - AX)
    second = forced_column(jax.random.fold_in(key, 12), SHOTS, MY - AY)
    return jnp.stack([first, second], axis=1).astype(jnp.int32)


def draw_source(key, part):
    return cell_rows(jax.random.fold_in(key, 21), SHOTS)


def draw_receivers(key, part):
    return cell_rows(jax.random.fold_in(key, 31), SHOTS * NREC).reshape(SHOTS, NREC, 3)


def levels(stream_key, shape, shards, smallest, largest):
    gain, own = 1.0, jax.random.fold_in(stream_key, 6)
    for axis_at, shards_of in shards:
        steps = jnp.exp(jax.random.uniform(jax.random.fold_in(own, axis_at), (shards_of,), jnp.float32, smallest / len(shards), largest / len(shards)))
        gain = gain * jnp.repeat(steps, shape[axis_at] // shards_of).reshape([-1 if axis == axis_at else 1 for axis in range(len(shape))])
    return gain


def scatter_about(rng, extent, width, most, cuts=(), held_as=jnp.bfloat16):
    drawn = width * jax.random.normal(rng, extent, jnp.float32)
    if cuts:
        drawn = drawn * levels(rng, extent, cuts, -0.22, 0.18)
    return jnp.clip(drawn, -most, most).astype(held_as)


def setup_inputs(seed: int = 0) -> dict:
    seeds = jax.random.split(jax.random.key(seed), 11)
    courant = jnp.clip(jnp.exp(math.log(0.18) - 1.2809339 * jax.random.uniform(seeds[0], (MX, MY, MZ), jnp.float32) ** levels(seeds[0], (MX, MY, MZ), ((0, 16), (1, 32)), -0.2, 0.2)), 0.05, 0.18)
    anchor = draw_anchor(jax.random.fold_in(seeds[10], 71), 0)
    source = draw_source(jax.random.fold_in(seeds[10], 71), 0)
    wavelet = scatter_about(seeds[3], (SHOTS, STEPS), 2.0, 12.0, ((0, 16),), jnp.float32)
    receivers = draw_receivers(jax.random.fold_in(seeds[10], 71), 0)
    observed = scatter_about(seeds[5], (SHOTS, STEPS, NREC), 0.5, 3.0, ((0, 16),), jnp.float32)
    wave_before = scatter_about(seeds[6], (SHOTS, AX, AY, MZ), 0.3, 1.8, ((0, 16), (1, 32)), jnp.float32)
    wave_now = scatter_about(seeds[7], (SHOTS, AX, AY, MZ), 0.3, 1.8, ((0, 16), (1, 32)), jnp.float32)
    adjoint_after = scatter_about(seeds[8], (SHOTS, AX, AY, MZ), 0.3, 1.8, ((0, 16), (1, 32)), jnp.float32)
    adjoint_now = scatter_about(seeds[9], (SHOTS, AX, AY, MZ), 0.3, 1.8, ((0, 16), (1, 32)), jnp.float32)
    return {"courant": courant, "anchor": anchor, "source": source, "wavelet": wavelet, "receivers": receivers, "observed": observed, "wave_before": wave_before, "wave_now": wave_now, "adjoint_after": adjoint_after, "adjoint_now": adjoint_now}


stencil_coef = (-205.0 / 72.0, 8.0 / 5.0, -1.0 / 5.0, 8.0 / 315.0, -1.0 / 560.0)


def stencil(padded, extent_x, extent_y, extent_z):
    def offset_view(shift_x, shift_y, shift_z):
        return padded[4 + shift_x:4 + shift_x + extent_x, 4 + shift_y:4 + shift_y + extent_y, 4 + shift_z:4 + shift_z + extent_z]

    total = (3.0 * stencil_coef[0]) * offset_view(0, 0, 0)
    for reach in range(1, 5):
        beside_all = offset_view(reach, 0, 0) + offset_view(-reach, 0, 0)
        beside_all = beside_all + offset_view(0, reach, 0) + offset_view(0, -reach, 0)
        beside_all = beside_all + offset_view(0, 0, reach) + offset_view(0, 0, -reach)
        total = total + stencil_coef[reach] * beside_all
    return total


def laplace(field):
    return stencil(jnp.pad(field, 4), field.shape[0], field.shape[1], field.shape[2])


def reference(courant, anchor, source, wavelet, receivers, observed, wave_before, wave_now, adjoint_after, adjoint_now):
    gradient = jnp.zeros((MX, MY, MZ), jnp.float32)
    zero_index = jnp.int32(0)
    for shot_index in range(SHOTS):
        corner_x = anchor[shot_index, 0].astype(jnp.int32)
        corner_y = anchor[shot_index, 1].astype(jnp.int32)
        speed_window = lax.dynamic_slice(courant, (corner_x, corner_y, zero_index), (AX, AY, MZ))
        source_cell = source[shot_index]
        receiver_cells = receivers[shot_index]
        previous = wave_before[shot_index]
        current = wave_now[shot_index]
        laplacians = []
        residuals = []
        for step_index in range(STEPS):
            laplace_now = laplace(current)
            laplacians.append(laplace_now)
            next_field = 2.0 * current - previous + speed_window * laplace_now
            next_field = next_field.at[source_cell[0], source_cell[1], source_cell[2]].add(wavelet[shot_index, step_index])
            recorded = next_field[receiver_cells[:, 0], receiver_cells[:, 1], receiver_cells[:, 2]]
            residuals.append(recorded - observed[shot_index, step_index])
            previous, current = current, next_field
        farther = adjoint_after[shot_index]
        nearer = adjoint_now[shot_index].at[receiver_cells[:, 0], receiver_cells[:, 1], receiver_cells[:, 2]].add(residuals[STEPS - 1])
        imaging = jnp.zeros((AX, AY, MZ), jnp.float32)
        for step_index in range(STEPS - 1, -1, -1):
            imaging = imaging + nearer * laplacians[step_index]
            if step_index > 0:
                updated = 2.0 * nearer - farther + laplace(speed_window * nearer)
                updated = updated.at[receiver_cells[:, 0], receiver_cells[:, 1], receiver_cells[:, 2]].add(residuals[step_index - 1])
                farther, nearer = nearer, updated
        block_now = lax.dynamic_slice(gradient, (corner_x, corner_y, zero_index), (AX, AY, MZ))
        gradient = lax.dynamic_update_slice(gradient, block_now + imaging, (corner_x, corner_y, zero_index))
    return gradient
```

```python
import jax
import jax.numpy as jnp
import numpy as np
from jax import lax
from jax.experimental import pallas as pl
from jax.experimental.pallas import tpu as pltpu
from jax.sharding import PartitionSpec as P

MESH = pl.DeviceIdType.MESH
HIGH = lax.Precision.HIGHEST
COEF = (-205.0 / 72.0, 8.0 / 5.0, -1.0 / 5.0, 8.0 / 315.0, -1.0 / 560.0)
F32 = jnp.float32
I32 = jnp.int32


def depth_band():
    cell = np.arange(128)
    apart = np.abs(cell[:, None] - cell[None, :])
    band = np.where(apart == 0, 3.0 * COEF[0], 0.0)
    for reach in range(1, 5):
        band = np.where(apart == reach, COEF[reach], band)
    return band.astype(np.float32)


def kernel(
    anchor, source, wavelet, band, receivers, observed, courant, wave_before, wave_now,
    adjoint_after, adjoint_now, out,
    gath, picked, rows, rowsend, cols, halfsend, half, twice, speed,
    pad, before, after_now, after, laps, third, adj, spot, images,
    back_half, back_in, back_send, back_rows, back_pick, back_in_x, back_sum, back_in_y,
    anchors, anchor_own,
    local_sem, field_send, field_recv, y_send, y_recv, a_send, a_recv, x_send, x_recv,
    s_send, s_recv, h_send, h_recv, halo_send, halo_recv,
    bh_send, bh_recv, bs_send, bs_recv, bx_send, bx_recv, by_send, by_recv,
):
    shot = lax.axis_index("shot")
    space = lax.axis_index("space")
    yl, x = shot // 4, shot % 4
    z, yh, c = space // 4, (space // 2) % 2, space % 2
    k = 2 * z + c

    def at_k(other):
        return (shot, (other // 2) * 4 + yh * 2 + other % 2)

    def at_x(other):
        return (yl * 4 + other, space)

    def at_y(other):
        return (other * 4 + x, space)

    partner = (shot, z * 4 + (1 - yh) * 2 + c)
    diagonal = (shot, z * 4 + (1 - yh) * 2 + (1 - c))

    def push(src, dst, send, recv, device):
        return pltpu.make_async_remote_copy(
            src_ref=src, dst_ref=dst, send_sem=send, recv_sem=recv,
            device_id=device, device_id_type=MESH,
        )

    def landed(dst, sem):
        pltpu.make_async_copy(dst, dst, sem).wait()

    for n in range(5):
        pad[n, 0:4] = jnp.zeros((4, 80, 128), F32)
        pad[n, 12:16] = jnp.zeros((4, 80, 128), F32)
        pad[n, 4:12, 0:8] = jnp.zeros((8, 8, 128), F32)
        pad[n, 4:12, 72:80] = jnp.zeros((8, 8, 128), F32)
    ox, oy = anchor[0, 0], anchor[0, 1]
    anchor_own[...] = jnp.full((8, 128), ox, I32)
    anchors[x] = jnp.full((8, 128), ox, I32)

    barrier = pltpu.get_barrier_semaphore()
    for d in range(1, 4):
        pl.semaphore_signal(barrier, 1, device_id=at_x((x + d) % 4), device_id_type=MESH)
        pl.semaphore_signal(barrier, 1, device_id=at_y((yl + d) % 4), device_id_type=MESH)
    for d in range(1, 16):
        pl.semaphore_signal(barrier, 1, device_id=at_k((k + d) % 16), device_id_type=MESH)
    pl.semaphore_signal(barrier, 1, device_id=partner, device_id_type=MESH)
    pl.semaphore_signal(barrier, 1, device_id=diagonal, device_id_type=MESH)
    pl.semaphore_wait(barrier, 23)

    def y_copy(d):
        return push(courant, gath.at[yl], y_send.at[d], y_recv.at[d], at_y((yl + d) % 4))

    own_model = pltpu.make_async_copy(courant, gath.at[yl], local_sem.at[0])
    own_model.start()
    for d in (1, 2, 3):
        y_copy(d).start()

    def a_copy(d):
        return push(anchor_own, anchors.at[x], a_send.at[d], a_recv.at[d], at_x((x + d) % 4))

    for d in (1, 2, 3):
        a_copy(d).start()

    def field_parts(n):
        src = (wave_now, wave_before, adjoint_now, adjoint_after)[n]

        def dst(core):
            if n == 0:
                return pad.at[0, pl.ds(4 + 4 * core, 4), pl.ds(8, 64)]
            return (before, after_now, after)[n - 1].at[pl.ds(4 * core, 4)]

        return src, dst

    def field_copy(n, h):
        src, dst = field_parts(n)
        return push(
            src.at[0, :, pl.ds(64 * h, 64), :], dst(c), field_send.at[n, h], field_recv.at[n, c],
            (shot, z * 4 + 2 * h + yh),
        )

    def stays(h):
        return jnp.logical_and(yh == h, c == h)

    def field_start(n):
        src, dst = field_parts(n)
        for h in range(2):

            @pl.when(stays(h))
            def _():
                pltpu.make_async_copy(
                    src.at[0, :, pl.ds(64 * h, 64), :], dst(c), field_recv.at[n, c]
                ).start()

            @pl.when(jnp.logical_not(stays(h)))
            def _():
                field_copy(n, h).start()

    def field_wait(n):
        src, dst = field_parts(n)
        for core in range(2):
            landed(dst(core), field_recv.at[n, core])

    field_start(0)
    field_start(1)

    row_of = receivers[0, :, 0:1] - 8 * k
    col_of = receivers[0, :, 1:2] - 64 * yh
    inside = (row_of >= 0) & (row_of < 8) & (col_of >= 0) & (col_of < 64)
    flat = jnp.where(inside, row_of * 64 + col_of, -1)
    hit = jnp.where(
        lax.broadcasted_iota(I32, (64, 512), 1) == flat, 1.0, 0.0
    ).astype(F32)
    deep = jnp.where(
        lax.broadcasted_iota(I32, (64, 128), 1) == receivers[0, :, 2:3], 1.0, 0.0
    ).astype(F32)
    square = lax.broadcasted_iota(I32, (64, 64), 0) == lax.broadcasted_iota(I32, (64, 64), 1)
    s_row, s_col, s_dep = source[0, 0] - 8 * k, source[0, 1] - 64 * yh, source[0, 2]
    spot[...] = jnp.where(
        (lax.broadcasted_iota(I32, (8, 64, 128), 0) == s_row)
        & (lax.broadcasted_iota(I32, (8, 64, 128), 1) == s_col)
        & (lax.broadcasted_iota(I32, (8, 64, 128), 2) == s_dep),
        1.0, 0.0,
    ).astype(F32)

    def record(field, n):
        lines = jnp.dot(hit, field.reshape(512, 128), precision=HIGH, preferred_element_type=F32)
        got = jnp.sum(lines * deep, axis=1, keepdims=True)
        seen = jnp.sum(
            jnp.where(square, jnp.broadcast_to(observed[0, n : n + 1, :], (64, 64)), 0.0),
            axis=1, keepdims=True,
        )
        return got - seen

    def inject(residual):
        return lax.dot_general(
            hit, deep * residual, (((0,), (0,)), ((), ())),
            precision=HIGH, preferred_element_type=F32,
        ).reshape(8, 64, 128)

    def halo_parts(n):
        up = push(
            pad.at[n, pl.ds(4, 4), pl.ds(8, 64)], pad.at[n, pl.ds(12, 4), pl.ds(8, 64)],
            halo_send.at[n, 0], halo_recv.at[n, 0], at_k((k + 15) % 16),
        )
        down = push(
            pad.at[n, pl.ds(8, 4), pl.ds(8, 64)], pad.at[n, pl.ds(0, 4), pl.ds(8, 64)],
            halo_send.at[n, 1], halo_recv.at[n, 1], at_k((k + 1) % 16),
        )
        side = push(
            pad.at[n, pl.ds(4, 8), pl.ds(pl.multiple_of(64 - 56 * yh, 8), 8)],
            pad.at[n, pl.ds(4, 8), pl.ds(pl.multiple_of(72 * yh, 8), 8)],
            halo_send.at[n, 2], halo_recv.at[n, 2], partner,
        )
        return up, down, side

    def halo_start(n):
        up, down, side = halo_parts(n)

        @pl.when(k > 0)
        def _():
            up.start()

        @pl.when(k < 15)
        def _():
            down.start()

        side.start()

    def halo_wait(n):
        @pl.when(k > 0)
        def _():
            landed(pad.at[n, pl.ds(0, 4), pl.ds(8, 64)], halo_recv.at[n, 1])

        @pl.when(k < 15)
        def _():
            landed(pad.at[n, pl.ds(12, 4), pl.ds(8, 64)], halo_recv.at[n, 0])

        landed(
            pad.at[n, pl.ds(4, 8), pl.ds(pl.multiple_of(72 - 72 * yh, 8), 8)], halo_recv.at[n, 2]
        )

    def halo_done(n):
        up, down, side = halo_parts(n)

        @pl.when(k > 0)
        def _():
            up.wait_send()

        @pl.when(k < 15)
        def _():
            down.wait_send()

        side.wait_send()

    def laplace(n):
        total = jnp.dot(
            pad[n, 4:12, 8:72].reshape(512, 128), band[...],
            precision=HIGH, preferred_element_type=F32,
        ).reshape(8, 64, 128)
        for d in range(1, 5):
            beside = pad[n, 4 - d : 12 - d, 8:72] + pad[n, 4 + d : 12 + d, 8:72]
            beside += pad[n, 4:12, 8 - d : 72 - d] + pad[n, 4:12, 8 + d : 72 + d]
            total += COEF[d] * beside
        return total

    field_wait(0)
    halo_start(0)

    own_model.wait()
    for d in (1, 2, 3):
        landed(gath.at[(yl + 4 - d) % 4], y_recv.at[d])
        landed(anchors.at[(x + 4 - d) % 4], a_recv.at[d])

    residue = 32 * x + lax.broadcasted_iota(I32, (32, 8, 128), 0)

    def super_of(other):
        start = anchors[other]
        return (start >> 7)[None] + jnp.where(residue < (start & 127)[None], 1, 0)

    def x_copy(d):
        return push(
            picked.at[d], rows.at[pl.ds(pl.multiple_of(32 * x, 32), 32)],
            x_send.at[d], x_recv.at[d], at_x((x + d) % 4),
        )

    for d in (2, 1, 3, 0):
        which = super_of((x + d) % 4)
        chosen = gath[0]
        for q in range(1, 4):
            chosen = jnp.where(which == q, gath[q], chosen)
        if d:
            picked[d] = chosen
            x_copy(d).start()
        else:
            rows[pl.ds(pl.multiple_of(32 * x, 32), 32)] = chosen

    halo_wait(0)
    laps[0] = laplace(0)

    for d in (1, 3, 2):
        landed(rows.at[pl.ds(pl.multiple_of(32 * ((x + 4 - d) % 4), 32), 32)], x_recv.at[d])

    first = ox & 127

    def s_copy(d):
        return push(rowsend.at[d], cols.at[k], s_send.at[d], s_recv.at[d], at_k((k + d) % 16))

    def spread(d, carry):
        other = (k + d) % 16
        for r in range(8):
            rowsend[d, r] = rows[(first + 8 * other + r) & 127]
        s_copy(d).start()
        return carry

    lax.fori_loop(1, 16, spread, 0)
    for r in range(8):
        cols[k, r] = rows[(first + 8 * k + r) & 127]

    field_start(2)
    field_start(3)

    def spread_in(d, carry):
        landed(cols.at[(k + 16 - d) % 16], s_recv.at[d])
        return carry

    lax.fori_loop(1, 16, spread_in, 0)

    turn = oy & 63
    lane_col = lax.broadcasted_iota(I32, (8, 8, 128), 1)

    def columns(h, e, core):
        at = (oy >> 6) + h
        place = 32 * e + 16 * yh + 8 * core + lane_col
        low = cols[4 * at + 2 * e + core]
        high = cols[4 * jnp.minimum(at + 1, 3) + 2 * e + core]
        return jnp.where(place < turn, high, low)

    h_copy = push(halfsend, half.at[yh], h_send, h_recv, partner)
    for e in range(2):
        for core in range(2):
            halfsend[e, core] = columns(1 - yh, e, core)
    h_copy.start()
    for e in range(2):
        for core in range(2):
            half[yh, e, core] = columns(yh, e, core)
    landed(half.at[1 - yh], h_recv)
    for e in range(2):
        for b in range(2):
            for core in range(2):
                t = 4 * e + 2 * b + core
                twice[:, 8 * t : 8 * t + 8] = half[b, e, core]
                twice[:, 64 + 8 * t : 72 + 8 * t] = half[b, e, core]
    for r in range(8):
        speed[r] = twice[r, pl.ds(turn, 64)]

    field_wait(1)
    now = pad[0, 4:12, 8:72]
    new = 2.0 * now - before[...] + speed[...] * laps[0] + wavelet[0, 0] * spot[...]
    pad[1, 4:12, 8:72] = new
    halo_start(1)
    residual0 = record(new, 0)
    halo_wait(1)
    lap = laplace(1)
    laps[1] = lap
    new = (
        2.0 * pad[1, 4:12, 8:72] - pad[0, 4:12, 8:72] + speed[...] * lap
        + wavelet[0, 1] * spot[...]
    )
    pad[2, 4:12, 8:72] = new
    halo_start(2)
    residual1 = record(new, 1)
    halo_wait(2)
    lap = laplace(2)
    laps[2] = lap
    new = (
        2.0 * pad[2, 4:12, 8:72] - pad[1, 4:12, 8:72] + speed[...] * lap
        + wavelet[0, 2] * spot[...]
    )
    third[...] = new
    residual2 = record(third[...], 2)

    field_wait(2)
    adj[0] = after_now[...] + inject(residual2)
    pad[3, 4:12, 8:72] = speed[...] * adj[0]
    halo_start(3)
    images[:, 0:64] = adj[0] * laps[2]
    field_wait(3)
    adj[1] = 2.0 * adj[0] - after[...] + inject(residual1)
    halo_wait(3)
    adj[1] = adj[1] + laplace(3)
    pad[4, 4:12, 8:72] = speed[...] * adj[1]
    halo_start(4)
    images[:, 0:64] = images[:, 0:64] + adj[1] * laps[1]
    third[...] = 2.0 * adj[1] - adj[0] + inject(residual0)
    halo_wait(4)
    image = images[:, 0:64] + (third[...] + laplace(4)) * laps[0]
    images[:, 0:64] = image
    images[:, 64:128] = image

    for r in range(8):
        line = images[r, pl.ds(64 - turn, 64)]
        for e in range(2):
            for b in range(2):
                for core in range(2):
                    t = 4 * e + 2 * b + core
                    back_half[b, e, core, r] = line[8 * t : 8 * t + 8]
    bh_copy = push(back_half.at[1 - yh], back_in, bh_send, bh_recv, partner)
    bh_copy.start()
    bh_copy.wait_recv()

    lane_row = lax.broadcasted_iota(I32, (8, 128), 0)

    def owned(other):
        zz, core = other // 2, other % 2
        e, q = zz % 2, zz // 2
        wraps = jnp.where(32 * e + 16 * yh + 8 * core + lane_row < turn, 1, 0)
        mine = (wraps + ((oy >> 6) + yh) == q)[None]
        theirs = (wraps + ((oy >> 6) + 1 - yh) == q)[None]
        return jnp.where(mine, back_half[yh, e, core], 0.0) + jnp.where(
            theirs, back_in[e, core], 0.0
        )

    def bs_copy(d):
        return push(
            back_send.at[d], back_rows.at[pl.ds(pl.multiple_of(8 * k, 8), 8)],
            bs_send.at[d], bs_recv.at[d], at_k((k + d) % 16),
        )

    def give(d, carry):
        back_send[d] = owned((k + d) % 16)
        bs_copy(d).start()
        return carry

    lax.fori_loop(1, 16, give, 0)
    back_rows[pl.ds(pl.multiple_of(8 * k, 8), 8)] = owned(k)

    def given(d, carry):
        landed(
            back_rows.at[pl.ds(pl.multiple_of(8 * ((k + 16 - d) % 16), 8), 8)], bs_recv.at[d]
        )
        return carry

    lax.fori_loop(1, 16, given, 0)

    def bx_copy(d):
        return push(
            back_pick.at[d], back_in_x.at[x], bx_send.at[d], bx_recv.at[d], at_x((x + d) % 4)
        )

    for d in (2, 1, 3, 0):
        other = (x + d) % 4

        def turned(i, carry):
            value = back_rows[(32 * other + i + 128 - first) & 127]
            back_pick[d, i] = value
            return carry

        lax.fori_loop(0, 32, turned, 0)
        if d:
            bx_copy(d).start()
        else:
            back_in_x[x] = back_pick[0]
    for d in (1, 3, 2):
        landed(back_in_x.at[(x + 4 - d) % 4], bx_recv.at[d])

    def by_copy(d):
        return push(
            back_sum.at[d], back_in_y.at[d], by_send.at[d], by_recv.at[d], at_y((yl + d) % 4)
        )

    for d in (2, 1, 3, 0):
        total = jnp.zeros((32, 8, 128), F32)
        for other in range(4):
            total += jnp.where(super_of(other) == (yl + d) % 4, back_in_x[other], 0.0)
        if d:
            back_sum[d] = total
            by_copy(d).start()
        else:
            back_sum[0] = total
    for d in (1, 2, 3):
        landed(back_in_y.at[d], by_recv.at[d])
    out[...] = back_sum[0] + back_in_y[1] + back_in_y[2] + back_in_y[3]

    for d in (1, 2, 3):
        y_copy(d).wait_send()
        a_copy(d).wait_send()
        x_copy(d).wait_send()
        bx_copy(d).wait_send()
        by_copy(d).wait_send()

    def left(d, carry):
        s_copy(d).wait_send()
        bs_copy(d).wait_send()
        return carry

    lax.fori_loop(1, 16, left, 0)
    h_copy.wait_send()
    bh_copy.wait_send()
    for n in range(5):
        halo_done(n)
    for n in range(4):
        for h in range(2):

            @pl.when(jnp.logical_not(stays(h)))
            def _():
                field_copy(n, h).wait_send()


def on_device(
    courant, anchor, source, wavelet, receivers, observed,
    wave_before, wave_now, adjoint_after, adjoint_now,
):
    vmem, smem, anywhere = pltpu.VMEM, pltpu.SMEM, pl.ANY
    dma = pltpu.SemaphoreType.DMA
    return pl.pallas_call(
        kernel,
        out_shape=jax.ShapeDtypeStruct((32, 8, 128), F32),
        in_specs=[pl.BlockSpec(memory_space=smem)] * 3
        + [pl.BlockSpec(memory_space=vmem)] * 3
        + [pl.BlockSpec(memory_space=anywhere)] * 5,
        out_specs=pl.BlockSpec(memory_space=vmem),
        scratch_shapes=[
            vmem((4, 32, 8, 128), F32),
            vmem((4, 32, 8, 128), F32),
            vmem((128, 8, 128), F32),
            vmem((16, 8, 8, 128), F32),
            vmem((16, 8, 8, 128), F32),
            vmem((2, 2, 8, 8, 128), F32),
            vmem((2, 2, 2, 8, 8, 128), F32),
            vmem((8, 128, 128), F32),
            vmem((8, 64, 128), F32),
            vmem((5, 16, 80, 128), F32),
            vmem((8, 64, 128), F32),
            vmem((8, 64, 128), F32),
            vmem((8, 64, 128), F32),
            vmem((3, 8, 64, 128), F32),
            vmem((8, 64, 128), F32),
            vmem((2, 8, 64, 128), F32),
            vmem((8, 64, 128), F32),
            vmem((8, 128, 128), F32),
            vmem((2, 2, 2, 8, 8, 128), F32),
            vmem((2, 2, 8, 8, 128), F32),
            vmem((16, 8, 8, 128), F32),
            vmem((128, 8, 128), F32),
            vmem((4, 32, 8, 128), F32),
            vmem((4, 32, 8, 128), F32),
            vmem((4, 32, 8, 128), F32),
            vmem((4, 32, 8, 128), F32),
            vmem((4, 8, 128), I32),
            vmem((8, 128), I32),
            dma((1,)),
            dma((4, 2)), dma((4, 2)),
            dma((4,)), dma((4,)),
            dma((4,)), dma((4,)),
            dma((4,)), dma((4,)),
            dma((16,)), dma((16,)),
            dma, dma,
            dma((5, 3)), dma((5, 3)),
            dma, dma,
            dma((16,)), dma((16,)),
            dma((4,)), dma((4,)),
            dma((4,)), dma((4,)),
        ],
        compiler_params=pltpu.CompilerParams(
            collective_id=0, has_side_effects=True, vmem_limit_bytes=40 * 1024 * 1024
        ),
    )(
        anchor, source, wavelet, jnp.asarray(depth_band()), receivers, observed, courant,
        wave_before, wave_now, adjoint_after, adjoint_now,
    )


def solution(mesh):
    return jax.shard_map(
        on_device,
        mesh=mesh,
        in_specs=(
            P("shot", "space", None),
            P("shot", None),
            P("shot", None),
            P("shot", None),
            P("shot", None, None),
            P("shot", None, None),
            P("shot", "space", None, None),
            P("shot", "space", None, None),
            P("shot", "space", None, None),
            P("shot", "space", None, None),
        ),
        out_specs=P("shot", "space", None),
        check_vma=False,
    )
```

```python
import jax
import jax.numpy as jnp
from jax import lax
from jax.experimental import pallas as pl
from jax.experimental.pallas import tpu as pltpu
from jax.sharding import PartitionSpec as P

MESH = pl.DeviceIdType.MESH
HIGH = lax.Precision.HIGHEST
COEF = (-205.0 / 72.0, 8.0 / 5.0, -1.0 / 5.0, 8.0 / 315.0, -1.0 / 560.0)
F32 = jnp.float32
I32 = jnp.int32


def kernel(
    anchor_in, source_in, wavelet_in, receivers_in, observed_in, courant, wave_before, wave_now,
    adjoint_after, adjoint_now, out,
    gath, picked, rows, rowsend, cols, halfsend, half, twice, speed,
    pad, before, after_now, after, laps, third, adj, spot, images,
    back_half, back_in, back_send, back_rows, back_pick, back_in_x, back_sum, back_in_y,
    anchors, anchor_own, anchor, source, wavelet, receivers, observed, band, hits, deeps, seens,
    local_sem, field_send, field_recv, y_send, y_recv, a_send, a_recv, x_send, x_recv,
    s_send, s_recv, h_send, h_recv, halo_send, halo_recv,
    bh_send, bh_recv, bs_send, bs_recv, bx_send, bx_recv, by_send, by_recv,
):
    shot = lax.axis_index("shot")
    space = lax.axis_index("space")
    yl, x = shot // 4, shot % 4
    z, yh, c = space // 4, (space // 2) % 2, space % 2
    k = 2 * z + c

    def at_k(other):
        return (shot, (other // 2) * 4 + yh * 2 + other % 2)

    def at_x(other):
        return (yl * 4 + other, space)

    def at_y(other):
        return (other * 4 + x, space)

    partner = (shot, z * 4 + (1 - yh) * 2 + c)
    diagonal = (shot, z * 4 + (1 - yh) * 2 + (1 - c))

    def push(src, dst, send, recv, device):
        return pltpu.make_async_remote_copy(
            src_ref=src, dst_ref=dst, send_sem=send, recv_sem=recv,
            device_id=device, device_id_type=MESH,
        )

    def landed(dst, sem):
        pltpu.make_async_copy(dst, dst, sem).wait()

    small = [
        pltpu.make_async_copy(src, dst, local_sem.at[1 + n])
        for n, (src, dst) in enumerate(
            (
                (anchor_in, anchor), (source_in, source), (wavelet_in, wavelet),
                (receivers_in, receivers), (observed_in, observed),
            )
        )
    ]
    for copy in small:
        copy.start()

    for n in range(5):
        pad[n, 0:4] = jnp.zeros((4, 80, 128), F32)
        pad[n, 12:16] = jnp.zeros((4, 80, 128), F32)
        pad[n, 4:12, 0:8] = jnp.zeros((8, 8, 128), F32)
        pad[n, 4:12, 72:80] = jnp.zeros((8, 8, 128), F32)
    for copy in small:
        copy.wait()
    ox, oy = anchor[0, 0], anchor[0, 1]
    anchor_own[...] = jnp.full((8, 128), ox, I32)
    anchors[x] = jnp.full((8, 128), ox, I32)

    barrier = pltpu.get_barrier_semaphore()
    for d in range(1, 4):
        pl.semaphore_signal(barrier, 1, device_id=at_x((x + d) % 4), device_id_type=MESH)
        pl.semaphore_signal(barrier, 1, device_id=at_y((yl + d) % 4), device_id_type=MESH)
    for d in range(1, 16):
        pl.semaphore_signal(barrier, 1, device_id=at_k((k + d) % 16), device_id_type=MESH)
    pl.semaphore_signal(barrier, 1, device_id=partner, device_id_type=MESH)
    pl.semaphore_signal(barrier, 1, device_id=diagonal, device_id_type=MESH)
    pl.semaphore_wait(barrier, 23)

    def y_copy(d):
        return push(courant, gath.at[yl], y_send.at[d], y_recv.at[d], at_y((yl + d) % 4))

    own_model = pltpu.make_async_copy(courant, gath.at[yl], local_sem.at[0])
    own_model.start()
    for d in (1, 2, 3):
        y_copy(d).start()

    def a_copy(d):
        return push(anchor_own, anchors.at[x], a_send.at[d], a_recv.at[d], at_x((x + d) % 4))

    for d in (1, 2, 3):
        a_copy(d).start()

    def field_parts(n):
        src = (wave_now, wave_before, adjoint_now, adjoint_after)[n]

        def dst(core):
            if n == 0:
                return pad.at[0, pl.ds(4 + 4 * core, 4), pl.ds(8, 64)]
            return (before, after_now, after)[n - 1].at[pl.ds(4 * core, 4)]

        return src, dst

    def field_copy(n, h):
        src, dst = field_parts(n)
        return push(
            src.at[0, :, pl.ds(64 * h, 64), :], dst(c), field_send.at[n, h], field_recv.at[n, c],
            (shot, z * 4 + 2 * h + yh),
        )

    def stays(h):
        return jnp.logical_and(yh == h, c == h)

    def field_start(n):
        src, dst = field_parts(n)
        for h in range(2):

            @pl.when(stays(h))
            def _():
                pltpu.make_async_copy(
                    src.at[0, :, pl.ds(64 * h, 64), :], dst(c), field_recv.at[n, c]
                ).start()

            @pl.when(jnp.logical_not(stays(h)))
            def _():
                field_copy(n, h).start()

    def field_wait(n):
        src, dst = field_parts(n)
        for core in range(2):
            landed(dst(core), field_recv.at[n, core])

    square = lax.broadcasted_iota(I32, (64, 64), 0) == lax.broadcasted_iota(I32, (64, 64), 1)

    def upright(row):
        return jnp.sum(
            jnp.where(square, jnp.broadcast_to(row.astype(F32), (64, 64)), 0.0),
            axis=1, keepdims=True,
        )

    row_of = receivers[0] - 8 * k
    col_of = receivers[1] - 64 * yh
    inside = (row_of >= 0) & (row_of < 8) & (col_of >= 0) & (col_of < 64)
    flat = upright(jnp.where(inside, row_of * 64 + col_of, -1))
    hits[...] = jnp.where(
        lax.broadcasted_iota(I32, (64, 512), 1).astype(F32) == flat, 1.0, 0.0
    ).astype(F32)
    deeps[...] = jnp.where(
        lax.broadcasted_iota(I32, (64, 128), 1).astype(F32) == upright(receivers[2]), 1.0, 0.0
    ).astype(F32)
    for n in range(3):
        seens[n] = upright(observed[n])
    apart = jnp.abs(
        lax.broadcasted_iota(I32, (128, 128), 0) - lax.broadcasted_iota(I32, (128, 128), 1)
    )
    line = jnp.where(apart == 0, 3.0 * COEF[0], 0.0)
    for reach in range(1, 5):
        line = jnp.where(apart == reach, COEF[reach], line)
    band[...] = line.astype(F32)
    s_row, s_col, s_dep = source[0, 0] - 8 * k, source[0, 1] - 64 * yh, source[0, 2]
    spot[...] = jnp.where(
        (lax.broadcasted_iota(I32, (8, 64, 128), 0) == s_row)
        & (lax.broadcasted_iota(I32, (8, 64, 128), 1) == s_col)
        & (lax.broadcasted_iota(I32, (8, 64, 128), 2) == s_dep),
        1.0, 0.0,
    ).astype(F32)

    def record(field, n):
        lines = jnp.dot(
            hits[...], field.reshape(512, 128), precision=HIGH, preferred_element_type=F32
        )
        return jnp.sum(lines * deeps[...], axis=1, keepdims=True) - seens[n]

    def inject(residual):
        return lax.dot_general(
            hits[...], deeps[...] * residual, (((0,), (0,)), ((), ())),
            precision=HIGH, preferred_element_type=F32,
        ).reshape(8, 64, 128)

    def halo_parts(n):
        up = push(
            pad.at[n, pl.ds(4, 4), pl.ds(8, 64)], pad.at[n, pl.ds(12, 4), pl.ds(8, 64)],
            halo_send.at[n, 0], halo_recv.at[n, 0], at_k((k + 15) % 16),
        )
        down = push(
            pad.at[n, pl.ds(8, 4), pl.ds(8, 64)], pad.at[n, pl.ds(0, 4), pl.ds(8, 64)],
            halo_send.at[n, 1], halo_recv.at[n, 1], at_k((k + 1) % 16),
        )
        side = push(
            pad.at[n, pl.ds(4, 8), pl.ds(pl.multiple_of(64 - 56 * yh, 8), 8)],
            pad.at[n, pl.ds(4, 8), pl.ds(pl.multiple_of(72 * yh, 8), 8)],
            halo_send.at[n, 2], halo_recv.at[n, 2], partner,
        )
        return up, down, side

    def halo_start(n):
        up, down, side = halo_parts(n)

        @pl.when(k > 0)
        def _():
            up.start()

        @pl.when(k < 15)
        def _():
            down.start()

        side.start()

    def halo_wait(n):
        @pl.when(k > 0)
        def _():
            landed(pad.at[n, pl.ds(0, 4), pl.ds(8, 64)], halo_recv.at[n, 1])

        @pl.when(k < 15)
        def _():
            landed(pad.at[n, pl.ds(12, 4), pl.ds(8, 64)], halo_recv.at[n, 0])

        landed(
            pad.at[n, pl.ds(4, 8), pl.ds(pl.multiple_of(72 - 72 * yh, 8), 8)], halo_recv.at[n, 2]
        )

    def halo_done(n):
        up, down, side = halo_parts(n)

        @pl.when(k > 0)
        def _():
            up.wait_send()

        @pl.when(k < 15)
        def _():
            down.wait_send()

        side.wait_send()

    def laplace(n):
        total = jnp.dot(
            pad[n, 4:12, 8:72].reshape(512, 128), band[...],
            precision=HIGH, preferred_element_type=F32,
        ).reshape(8, 64, 128)
        for d in range(1, 5):
            beside = pad[n, 4 - d : 12 - d, 8:72] + pad[n, 4 + d : 12 + d, 8:72]
            beside += pad[n, 4:12, 8 - d : 72 - d] + pad[n, 4:12, 8 + d : 72 + d]
            total += COEF[d] * beside
        return total

    own_model.wait()
    for d in (1, 2, 3):
        landed(gath.at[(yl + 4 - d) % 4], y_recv.at[d])
        landed(anchors.at[(x + 4 - d) % 4], a_recv.at[d])

    field_start(0)
    field_start(1)

    residue = 32 * x + lax.broadcasted_iota(I32, (32, 8, 128), 0)

    def super_of(other):
        start = anchors[other]
        return (start >> 7)[None] + jnp.where(residue < (start & 127)[None], 1, 0)

    def x_copy(d):
        return push(
            picked.at[d], rows.at[pl.ds(pl.multiple_of(32 * x, 32), 32)],
            x_send.at[d], x_recv.at[d], at_x((x + d) % 4),
        )

    for d in (2, 1, 3, 0):
        which = super_of((x + d) % 4)
        chosen = gath[0]
        for q in range(1, 4):
            chosen = jnp.where(which == q, gath[q], chosen)
        if d:
            picked[d] = chosen
            x_copy(d).start()
        else:
            rows[pl.ds(pl.multiple_of(32 * x, 32), 32)] = chosen

    for d in (1, 3, 2):
        landed(rows.at[pl.ds(pl.multiple_of(32 * ((x + 4 - d) % 4), 32), 32)], x_recv.at[d])

    first = ox & 127

    def s_copy(d):
        return push(rowsend.at[d], cols.at[k], s_send.at[d], s_recv.at[d], at_k((k + d) % 16))

    def spread(d, carry):
        other = (k + d) % 16
        for r in range(8):
            rowsend[d, r] = rows[(first + 8 * other + r) & 127]
        s_copy(d).start()
        return carry

    lax.fori_loop(1, 16, spread, 0)
    for r in range(8):
        cols[k, r] = rows[(first + 8 * k + r) & 127]

    field_start(2)
    field_start(3)

    field_wait(0)
    halo_start(0)
    halo_wait(0)
    laps[0] = laplace(0)

    def spread_in(d, carry):
        landed(cols.at[(k + 16 - d) % 16], s_recv.at[d])
        return carry

    lax.fori_loop(1, 16, spread_in, 0)

    turn = oy & 63
    lane_col = lax.broadcasted_iota(I32, (8, 8, 128), 1)

    def columns(h, e, core):
        at = (oy >> 6) + h
        place = 32 * e + 16 * yh + 8 * core + lane_col
        low = cols[4 * at + 2 * e + core]
        high = cols[4 * jnp.minimum(at + 1, 3) + 2 * e + core]
        return jnp.where(place < turn, high, low)

    h_copy = push(halfsend, half.at[yh], h_send, h_recv, partner)
    for e in range(2):
        for core in range(2):
            halfsend[e, core] = columns(1 - yh, e, core)
    h_copy.start()
    for e in range(2):
        for core in range(2):
            half[yh, e, core] = columns(yh, e, core)
    landed(half.at[1 - yh], h_recv)
    for e in range(2):
        for b in range(2):
            for core in range(2):
                t = 4 * e + 2 * b + core
                twice[:, 8 * t : 8 * t + 8] = half[b, e, core]
                twice[:, 64 + 8 * t : 72 + 8 * t] = half[b, e, core]
    for r in range(8):
        speed[r] = twice[r, pl.ds(turn, 64)]

    field_wait(1)
    now = pad[0, 4:12, 8:72]
    new = 2.0 * now - before[...] + speed[...] * laps[0] + wavelet[0, 0] * spot[...]
    pad[1, 4:12, 8:72] = new
    halo_start(1)
    residual0 = record(new, 0)
    halo_wait(1)
    lap = laplace(1)
    laps[1] = lap
    new = (
        2.0 * pad[1, 4:12, 8:72] - pad[0, 4:12, 8:72] + speed[...] * lap
        + wavelet[0, 1] * spot[...]
    )
    pad[2, 4:12, 8:72] = new
    halo_start(2)
    residual1 = record(new, 1)
    halo_wait(2)
    lap = laplace(2)
    laps[2] = lap
    new = (
        2.0 * pad[2, 4:12, 8:72] - pad[1, 4:12, 8:72] + speed[...] * lap
        + wavelet[0, 2] * spot[...]
    )
    third[...] = new
    residual2 = record(third[...], 2)

    field_wait(2)
    adj[0] = after_now[...] + inject(residual2)
    pad[3, 4:12, 8:72] = speed[...] * adj[0]
    halo_start(3)
    images[:, 0:64] = adj[0] * laps[2]
    field_wait(3)
    adj[1] = 2.0 * adj[0] - after[...] + inject(residual1)
    halo_wait(3)
    adj[1] = adj[1] + laplace(3)
    pad[4, 4:12, 8:72] = speed[...] * adj[1]
    halo_start(4)
    images[:, 0:64] = images[:, 0:64] + adj[1] * laps[1]
    third[...] = 2.0 * adj[1] - adj[0] + inject(residual0)
    halo_wait(4)
    image = images[:, 0:64] + (third[...] + laplace(4)) * laps[0]
    images[:, 0:64] = image
    images[:, 64:128] = image

    for r in range(8):
        line = images[r, pl.ds(64 - turn, 64)]
        for e in range(2):
            for b in range(2):
                for core in range(2):
                    t = 4 * e + 2 * b + core
                    back_half[b, e, core, r] = line[8 * t : 8 * t + 8]
    bh_copy = push(back_half.at[1 - yh], back_in, bh_send, bh_recv, partner)
    bh_copy.start()
    bh_copy.wait_recv()

    lane_row = lax.broadcasted_iota(I32, (8, 128), 0)

    def owned(other):
        zz, core = other // 2, other % 2
        e, q = zz % 2, zz // 2
        wraps = jnp.where(32 * e + 16 * yh + 8 * core + lane_row < turn, 1, 0)
        mine = (wraps + ((oy >> 6) + yh) == q)[None]
        theirs = (wraps + ((oy >> 6) + 1 - yh) == q)[None]
        return jnp.where(mine, back_half[yh, e, core], 0.0) + jnp.where(
            theirs, back_in[e, core], 0.0
        )

    def bs_copy(d):
        return push(
            back_send.at[d], back_rows.at[pl.ds(pl.multiple_of(8 * k, 8), 8)],
            bs_send.at[d], bs_recv.at[d], at_k((k + d) % 16),
        )

    def give(d, carry):
        back_send[d] = owned((k + d) % 16)
        bs_copy(d).start()
        return carry

    lax.fori_loop(1, 16, give, 0)
    back_rows[pl.ds(pl.multiple_of(8 * k, 8), 8)] = owned(k)

    def given(d, carry):
        landed(
            back_rows.at[pl.ds(pl.multiple_of(8 * ((k + 16 - d) % 16), 8), 8)], bs_recv.at[d]
        )
        return carry

    lax.fori_loop(1, 16, given, 0)

    def bx_copy(d):
        return push(
            back_pick.at[d], back_in_x.at[x], bx_send.at[d], bx_recv.at[d], at_x((x + d) % 4)
        )

    for d in (2, 1, 3, 0):
        other = (x + d) % 4

        def turned(i, carry):
            value = back_rows[(32 * other + i + 128 - first) & 127]
            back_pick[d, i] = value
            return carry

        lax.fori_loop(0, 32, turned, 0)
        if d:
            bx_copy(d).start()
        else:
            back_in_x[x] = back_pick[0]
    for d in (1, 3, 2):
        landed(back_in_x.at[(x + 4 - d) % 4], bx_recv.at[d])

    def by_copy(d):
        return push(
            back_sum.at[d], back_in_y.at[d], by_send.at[d], by_recv.at[d], at_y((yl + d) % 4)
        )

    for d in (2, 1, 3, 0):
        total = jnp.zeros((32, 8, 128), F32)
        for other in range(4):
            total += jnp.where(super_of(other) == (yl + d) % 4, back_in_x[other], 0.0)
        if d:
            back_sum[d] = total
            by_copy(d).start()
        else:
            back_sum[0] = total
    for d in (1, 2, 3):
        landed(back_in_y.at[d], by_recv.at[d])
    out[...] = back_sum[0] + back_in_y[1] + back_in_y[2] + back_in_y[3]

    for d in (1, 2, 3):
        y_copy(d).wait_send()
        a_copy(d).wait_send()
        x_copy(d).wait_send()
        bx_copy(d).wait_send()
        by_copy(d).wait_send()

    def left(d, carry):
        s_copy(d).wait_send()
        bs_copy(d).wait_send()
        return carry

    lax.fori_loop(1, 16, left, 0)
    h_copy.wait_send()
    bh_copy.wait_send()
    for n in range(5):
        halo_done(n)
    for n in range(4):
        for h in range(2):

            @pl.when(jnp.logical_not(stays(h)))
            def _():
                field_copy(n, h).wait_send()


def on_device(
    courant, anchor, source, wavelet, receivers, observed,
    wave_before, wave_now, adjoint_after, adjoint_now,
):
    vmem, smem = pltpu.VMEM, pltpu.SMEM
    dma = pltpu.SemaphoreType.DMA
    return pl.pallas_call(
        kernel,
        out_shape=jax.ShapeDtypeStruct((32, 8, 128), F32),
        in_specs=[pl.BlockSpec(memory_space=pltpu.HBM)] * 10,
        out_specs=pl.BlockSpec(memory_space=vmem),
        scratch_shapes=[
            vmem((4, 32, 8, 128), F32),
            vmem((4, 32, 8, 128), F32),
            vmem((128, 8, 128), F32),
            vmem((16, 8, 8, 128), F32),
            vmem((16, 8, 8, 128), F32),
            vmem((2, 2, 8, 8, 128), F32),
            vmem((2, 2, 2, 8, 8, 128), F32),
            vmem((8, 128, 128), F32),
            vmem((8, 64, 128), F32),
            vmem((5, 16, 80, 128), F32),
            vmem((8, 64, 128), F32),
            vmem((8, 64, 128), F32),
            vmem((8, 64, 128), F32),
            vmem((3, 8, 64, 128), F32),
            vmem((8, 64, 128), F32),
            vmem((2, 8, 64, 128), F32),
            vmem((8, 64, 128), F32),
            vmem((8, 128, 128), F32),
            vmem((2, 2, 2, 8, 8, 128), F32),
            vmem((2, 2, 8, 8, 128), F32),
            vmem((16, 8, 8, 128), F32),
            vmem((128, 8, 128), F32),
            vmem((4, 32, 8, 128), F32),
            vmem((4, 32, 8, 128), F32),
            vmem((4, 32, 8, 128), F32),
            vmem((4, 32, 8, 128), F32),
            vmem((4, 8, 128), I32),
            vmem((8, 128), I32),
            smem((1, 2), I32),
            smem((1, 3), I32),
            smem((1, 3), F32),
            vmem((3, 1, 64), I32),
            vmem((3, 1, 64), F32),
            vmem((128, 128), F32),
            vmem((64, 512), F32),
            vmem((64, 128), F32),
            vmem((3, 64, 1), F32),
            dma((6,)),
            dma((4, 2)), dma((4, 2)),
            dma((4,)), dma((4,)),
            dma((4,)), dma((4,)),
            dma((4,)), dma((4,)),
            dma((16,)), dma((16,)),
            dma, dma,
            dma((5, 3)), dma((5, 3)),
            dma, dma,
            dma((16,)), dma((16,)),
            dma((4,)), dma((4,)),
            dma((4,)), dma((4,)),
        ],
        compiler_params=pltpu.CompilerParams(
            collective_id=0, has_side_effects=True, vmem_limit_bytes=60 * 1024 * 1024
        ),
    )(
        anchor, source, wavelet, receivers.transpose(2, 0, 1), observed.transpose(1, 0, 2), courant,
        wave_before, wave_now, adjoint_after, adjoint_now,
    )


def solution(mesh):
    return jax.shard_map(
        on_device,
        mesh=mesh,
        in_specs=(
            P("shot", "space", None),
            P("shot", None),
            P("shot", None),
            P("shot", None),
            P("shot", None, None),
            P("shot", None, None),
            P("shot", "space", None, None),
            P("shot", "space", None, None),
            P("shot", "space", None, None),
            P("shot", "space", None, None),
        ),
        out_specs=P("shot", "space", None),
        check_vma=False,
    )
```

```python
import jax
import jax.numpy as jnp
from jax import lax
from jax.experimental import pallas as pl
from jax.experimental.pallas import tpu as pltpu
from jax.sharding import PartitionSpec as P

MESH = pl.DeviceIdType.MESH
HIGH = lax.Precision.HIGHEST
COEF = (-205.0 / 72.0, 8.0 / 5.0, -1.0 / 5.0, 8.0 / 315.0, -1.0 / 560.0)
F32 = jnp.float32
I32 = jnp.int32
PARTS = 2
WIDE = 8 // PARTS


def kernel(
    anchor_in, source_in, wavelet_in, receivers_in, observed_in, courant, wave_before, wave_now,
    adjoint_after, adjoint_now, out,
    gath, picked, rows_0, rows_1, rowsend, cols_0, cols_1, halfsend, half, twice, speed,
    pad, before, after_now, after, laps, third, adj, spot, images,
    back_half, back_in, back_send, back_rows_0, back_rows_1, back_pick, back_in_x, back_sum, back_in_y,
    anchors, anchor_own, anchor, source, wavelet, receivers, observed, band, hits, deeps, seens,
    local_sem, field_send, field_recv, y_send, y_recv, a_send, a_recv, x_send, x_recv,
    s_send, s_recv, h_send, h_recv, halo_send, halo_recv,
    bh_send, bh_recv, bs_send, bs_recv, bx_send, bx_recv, by_send, by_recv,
):
    rows, cols, back_rows = (rows_0, rows_1), (cols_0, cols_1), (back_rows_0, back_rows_1)
    shot = lax.axis_index("shot")
    space = lax.axis_index("space")
    yl, x = shot // 4, shot % 4
    z, yh, c = space // 4, (space // 2) % 2, space % 2
    k = 2 * z + c

    def at_k(other):
        return (shot, (other // 2) * 4 + yh * 2 + other % 2)

    def at_x(other):
        return (yl * 4 + other, space)

    def at_y(other):
        return (other * 4 + x, space)

    partner = (shot, z * 4 + (1 - yh) * 2 + c)
    diagonal = (shot, z * 4 + (1 - yh) * 2 + (1 - c))

    def push(src, dst, send, recv, device):
        return pltpu.make_async_remote_copy(
            src_ref=src, dst_ref=dst, send_sem=send, recv_sem=recv,
            device_id=device, device_id_type=MESH,
        )

    def landed(dst, sem):
        pltpu.make_async_copy(dst, dst, sem).wait()

    small = [
        pltpu.make_async_copy(src, dst, local_sem.at[1 + n])
        for n, (src, dst) in enumerate(
            (
                (anchor_in, anchor), (source_in, source), (wavelet_in, wavelet),
                (receivers_in, receivers), (observed_in, observed),
            )
        )
    ]
    for copy in small:
        copy.start()

    for n in range(5):
        pad[n, 0:4] = jnp.zeros((4, 80, 128), F32)
        pad[n, 12:16] = jnp.zeros((4, 80, 128), F32)
        pad[n, 4:12, 0:8] = jnp.zeros((8, 8, 128), F32)
        pad[n, 4:12, 72:80] = jnp.zeros((8, 8, 128), F32)
    for copy in small:
        copy.wait()
    ox, oy = anchor[0, 0], anchor[0, 1]
    anchor_own[...] = jnp.full((8, 128), ox, I32)
    anchors[x] = jnp.full((8, 128), ox, I32)

    barrier = pltpu.get_barrier_semaphore()
    for d in range(1, 4):
        pl.semaphore_signal(barrier, 1, device_id=at_x((x + d) % 4), device_id_type=MESH)
        pl.semaphore_signal(barrier, 1, device_id=at_y((yl + d) % 4), device_id_type=MESH)
    for d in range(1, 16):
        pl.semaphore_signal(barrier, 1, device_id=at_k((k + d) % 16), device_id_type=MESH)
    pl.semaphore_signal(barrier, 1, device_id=partner, device_id_type=MESH)
    pl.semaphore_signal(barrier, 1, device_id=diagonal, device_id_type=MESH)
    pl.semaphore_wait(barrier, 23)

    def part(g):
        return pl.ds(WIDE * g, WIDE)

    def y_copy(g, d):
        return push(
            courant.at[:, part(g), :], gath.at[yl, :, part(g), :],
            y_send.at[g, d], y_recv.at[g, d], at_y((yl + d) % 4),
        )

    own_model = pltpu.make_async_copy(courant, gath.at[yl], local_sem.at[0])
    own_model.start()

    def a_copy(d):
        return push(anchor_own, anchors.at[x], a_send.at[d], a_recv.at[d], at_x((x + d) % 4))

    for d in (1, 2, 3):
        a_copy(d).start()
    for g in range(PARTS):
        for d in (2, 1, 3):
            y_copy(g, d).start()

    def field_parts(n):
        src = (wave_now, wave_before, adjoint_now, adjoint_after)[n]

        def dst(core):
            if n == 0:
                return pad.at[0, pl.ds(4 + 4 * core, 4), pl.ds(8, 64)]
            return (before, after_now, after)[n - 1].at[pl.ds(4 * core, 4)]

        return src, dst

    def field_copy(n, h):
        src, dst = field_parts(n)
        return push(
            src.at[0, :, pl.ds(64 * h, 64), :], dst(c), field_send.at[n, h], field_recv.at[n, c],
            (shot, z * 4 + 2 * h + yh),
        )

    def stays(h):
        return jnp.logical_and(yh == h, c == h)

    def field_start(n):
        src, dst = field_parts(n)
        for h in range(2):

            @pl.when(stays(h))
            def _():
                pltpu.make_async_copy(
                    src.at[0, :, pl.ds(64 * h, 64), :], dst(c), field_recv.at[n, c]
                ).start()

            @pl.when(jnp.logical_not(stays(h)))
            def _():
                field_copy(n, h).start()

    def field_wait(n):
        src, dst = field_parts(n)
        for core in range(2):
            landed(dst(core), field_recv.at[n, core])

    square = lax.broadcasted_iota(I32, (64, 64), 0) == lax.broadcasted_iota(I32, (64, 64), 1)

    def upright(row):
        return jnp.sum(
            jnp.where(square, jnp.broadcast_to(row.astype(F32), (64, 64)), 0.0),
            axis=1, keepdims=True,
        )

    row_of = receivers[0] - 8 * k
    col_of = receivers[1] - 64 * yh
    inside = (row_of >= 0) & (row_of < 8) & (col_of >= 0) & (col_of < 64)
    flat = upright(jnp.where(inside, row_of * 64 + col_of, -1))
    hits[...] = jnp.where(
        lax.broadcasted_iota(I32, (64, 512), 1).astype(F32) == flat, 1.0, 0.0
    ).astype(F32)
    deeps[...] = jnp.where(
        lax.broadcasted_iota(I32, (64, 128), 1).astype(F32) == upright(receivers[2]), 1.0, 0.0
    ).astype(F32)
    for n in range(3):
        seens[n] = upright(observed[n])
    apart = jnp.abs(
        lax.broadcasted_iota(I32, (128, 128), 0) - lax.broadcasted_iota(I32, (128, 128), 1)
    )
    line = jnp.where(apart == 0, 3.0 * COEF[0], 0.0)
    for reach in range(1, 5):
        line = jnp.where(apart == reach, COEF[reach], line)
    band[...] = line.astype(F32)
    s_row, s_col, s_dep = source[0, 0] - 8 * k, source[0, 1] - 64 * yh, source[0, 2]
    spot[...] = jnp.where(
        (lax.broadcasted_iota(I32, (8, 64, 128), 0) == s_row)
        & (lax.broadcasted_iota(I32, (8, 64, 128), 1) == s_col)
        & (lax.broadcasted_iota(I32, (8, 64, 128), 2) == s_dep),
        1.0, 0.0,
    ).astype(F32)

    def record(field, n):
        lines = jnp.dot(
            hits[...], field.reshape(512, 128), precision=HIGH, preferred_element_type=F32
        )
        return jnp.sum(lines * deeps[...], axis=1, keepdims=True) - seens[n]

    def inject(residual):
        return lax.dot_general(
            hits[...], deeps[...] * residual, (((0,), (0,)), ((), ())),
            precision=HIGH, preferred_element_type=F32,
        ).reshape(8, 64, 128)

    def halo_parts(n):
        up = push(
            pad.at[n, pl.ds(4, 4), pl.ds(8, 64)], pad.at[n, pl.ds(12, 4), pl.ds(8, 64)],
            halo_send.at[n, 0], halo_recv.at[n, 0], at_k((k + 15) % 16),
        )
        down = push(
            pad.at[n, pl.ds(8, 4), pl.ds(8, 64)], pad.at[n, pl.ds(0, 4), pl.ds(8, 64)],
            halo_send.at[n, 1], halo_recv.at[n, 1], at_k((k + 1) % 16),
        )
        side = push(
            pad.at[n, pl.ds(4, 8), pl.ds(pl.multiple_of(64 - 56 * yh, 8), 8)],
            pad.at[n, pl.ds(4, 8), pl.ds(pl.multiple_of(72 * yh, 8), 8)],
            halo_send.at[n, 2], halo_recv.at[n, 2], partner,
        )
        return up, down, side

    def halo_start(n):
        up, down, side = halo_parts(n)

        @pl.when(k > 0)
        def _():
            up.start()

        @pl.when(k < 15)
        def _():
            down.start()

        side.start()

    def halo_wait(n):
        @pl.when(k > 0)
        def _():
            landed(pad.at[n, pl.ds(0, 4), pl.ds(8, 64)], halo_recv.at[n, 1])

        @pl.when(k < 15)
        def _():
            landed(pad.at[n, pl.ds(12, 4), pl.ds(8, 64)], halo_recv.at[n, 0])

        landed(
            pad.at[n, pl.ds(4, 8), pl.ds(pl.multiple_of(72 - 72 * yh, 8), 8)], halo_recv.at[n, 2]
        )

    def halo_done(n):
        up, down, side = halo_parts(n)

        @pl.when(k > 0)
        def _():
            up.wait_send()

        @pl.when(k < 15)
        def _():
            down.wait_send()

        side.wait_send()

    def laplace(n):
        total = jnp.dot(
            pad[n, 4:12, 8:72].reshape(512, 128), band[...],
            precision=HIGH, preferred_element_type=F32,
        ).reshape(8, 64, 128)
        for d in range(1, 5):
            beside = pad[n, 4 - d : 12 - d, 8:72] + pad[n, 4 + d : 12 + d, 8:72]
            beside += pad[n, 4:12, 8 - d : 72 - d] + pad[n, 4:12, 8 + d : 72 + d]
            total += COEF[d] * beside
        return total

    own_model.wait()
    for d in (1, 2, 3):
        landed(anchors.at[(x + 4 - d) % 4], a_recv.at[d])

    def super_of(other, g):
        start = anchors[other, part(g), :]
        residue = 32 * x + lax.broadcasted_iota(I32, (32, WIDE, 128), 0)
        return (start >> 7)[None] + jnp.where(residue < (start & 127)[None], 1, 0)

    def x_copy(g, d):
        return push(
            picked.at[d, :, part(g), :],
            rows[g].at[pl.ds(pl.multiple_of(32 * x, 32), 32), part(g), :],
            x_send.at[g, d], x_recv.at[g, d], at_x((x + d) % 4),
        )

    for g in range(PARTS):
        for d in (1, 3, 2):
            landed(gath.at[(yl + 4 - d) % 4, :, part(g), :], y_recv.at[g, d])
        for d in (2, 1, 3, 0):
            which = super_of((x + d) % 4, g)
            chosen = gath[0, :, part(g), :]
            for q in range(1, 4):
                chosen = jnp.where(which == q, gath[q, :, part(g), :], chosen)
            if d:
                picked[d, :, part(g), :] = chosen
                x_copy(g, d).start()
            else:
                rows[g][pl.ds(pl.multiple_of(32 * x, 32), 32), part(g), :] = chosen
    field_start(0)
    field_start(1)

    first = ox & 127

    def s_copy(g, d):
        return push(
            rowsend.at[d, :, part(g), :], cols[g].at[k, :, part(g), :],
            s_send.at[g, d], s_recv.at[g, d], at_k((k + d) % 16),
        )

    for g in range(PARTS):
        for d in (1, 3, 2):
            landed(
                rows[g].at[pl.ds(pl.multiple_of(32 * ((x + 4 - d) % 4), 32), 32), part(g), :],
                x_recv.at[g, d],
            )

        def spread(n, carry):
            d = (n + 8) % 16
            other = (k + d) % 16
            for r in range(8):
                rowsend[d, r, part(g), :] = rows[g][(first + 8 * other + r) & 127, part(g), :]
            s_copy(g, d).start()
            return carry

        lax.fori_loop(0, 8, spread, 0)
        lax.fori_loop(9, 16, spread, 0)
        for r in range(8):
            cols[g][k, r, part(g), :] = rows[g][(first + 8 * k + r) & 127, part(g), :]

    turn = oy & 63

    def columns(h, e, core, g):
        at = (oy >> 6) + h
        place = 32 * e + 16 * yh + 8 * core + WIDE * g + lax.broadcasted_iota(I32, (8, WIDE, 128), 1)
        low = cols[g][4 * at + 2 * e + core, :, part(g), :]
        high = cols[g][4 * jnp.minimum(at + 1, 3) + 2 * e + core, :, part(g), :]
        return jnp.where(place < turn, high, low)

    def h_copy(g):
        return push(
            halfsend.at[:, :, :, part(g), :], half.at[yh, :, :, :, part(g), :],
            h_send.at[g], h_recv.at[g], partner,
        )

    for g in range(PARTS):

        def spread_in(d, carry):
            landed(cols[g].at[(k + 16 - d) % 16, :, part(g), :], s_recv.at[g, d])
            return carry

        lax.fori_loop(1, 16, spread_in, 0)
        for e in range(2):
            for core in range(2):
                halfsend[e, core, :, part(g), :] = columns(1 - yh, e, core, g)
        h_copy(g).start()
        for e in range(2):
            for core in range(2):
                half[yh, e, core, :, part(g), :] = columns(yh, e, core, g)
        if g == 0:
            field_wait(0)
            halo_start(0)
    field_start(2)
    field_start(3)
    halo_wait(0)
    laps[0] = laplace(0)
    for g in range(PARTS):
        landed(half.at[1 - yh, :, :, :, part(g), :], h_recv.at[g])
    for e in range(2):
        for b in range(2):
            for core in range(2):
                t = 4 * e + 2 * b + core
                twice[:, 8 * t : 8 * t + 8] = half[b, e, core]
                twice[:, 64 + 8 * t : 72 + 8 * t] = half[b, e, core]
    for r in range(8):
        speed[r] = twice[r, pl.ds(turn, 64)]

    field_wait(1)
    now = pad[0, 4:12, 8:72]
    new = 2.0 * now - before[...] + speed[...] * laps[0] + wavelet[0, 0] * spot[...]
    pad[1, 4:12, 8:72] = new
    halo_start(1)
    residual0 = record(new, 0)
    halo_wait(1)
    lap = laplace(1)
    laps[1] = lap
    new = (
        2.0 * pad[1, 4:12, 8:72] - pad[0, 4:12, 8:72] + speed[...] * lap
        + wavelet[0, 1] * spot[...]
    )
    pad[2, 4:12, 8:72] = new
    halo_start(2)
    residual1 = record(new, 1)
    halo_wait(2)
    lap = laplace(2)
    laps[2] = lap
    new = (
        2.0 * pad[2, 4:12, 8:72] - pad[1, 4:12, 8:72] + speed[...] * lap
        + wavelet[0, 2] * spot[...]
    )
    third[...] = new
    residual2 = record(third[...], 2)

    field_wait(2)
    adj[0] = after_now[...] + inject(residual2)
    pad[3, 4:12, 8:72] = speed[...] * adj[0]
    halo_start(3)
    images[:, 0:64] = adj[0] * laps[2]
    field_wait(3)
    adj[1] = 2.0 * adj[0] - after[...] + inject(residual1)
    halo_wait(3)
    adj[1] = adj[1] + laplace(3)
    pad[4, 4:12, 8:72] = speed[...] * adj[1]
    halo_start(4)
    images[:, 0:64] = images[:, 0:64] + adj[1] * laps[1]
    third[...] = 2.0 * adj[1] - adj[0] + inject(residual0)
    halo_wait(4)
    image = images[:, 0:64] + (third[...] + laplace(4)) * laps[0]
    images[:, 0:64] = image
    images[:, 64:128] = image

    for r in range(8):
        line = images[r, pl.ds(64 - turn, 64)]
        for e in range(2):
            for b in range(2):
                for core in range(2):
                    t = 4 * e + 2 * b + core
                    back_half[b, e, core, r] = line[8 * t : 8 * t + 8]

    def bh_copy(g):
        return push(
            back_half.at[1 - yh, :, :, :, part(g), :], back_in.at[:, :, :, part(g), :],
            bh_send.at[g], bh_recv.at[g], partner,
        )

    for g in range(PARTS):
        bh_copy(g).start()

    def owned(other, g):
        zz, core = other // 2, other % 2
        e, q = zz % 2, zz // 2
        place = 32 * e + 16 * yh + 8 * core + WIDE * g + lax.broadcasted_iota(I32, (WIDE, 128), 0)
        wraps = jnp.where(place < turn, 1, 0)
        mine = (wraps + ((oy >> 6) + yh) == q)[None]
        theirs = (wraps + ((oy >> 6) + 1 - yh) == q)[None]
        return jnp.where(mine, back_half[yh, e, core, :, part(g), :], 0.0) + jnp.where(
            theirs, back_in[e, core, :, part(g), :], 0.0
        )

    def bs_copy(g, d):
        return push(
            back_send.at[d, :, part(g), :],
            back_rows[g].at[pl.ds(pl.multiple_of(8 * k, 8), 8), part(g), :],
            bs_send.at[g, d], bs_recv.at[g, d], at_k((k + d) % 16),
        )

    for g in range(PARTS):
        landed(back_in.at[:, :, :, part(g), :], bh_recv.at[g])

        def give(n, carry):
            d = (n + 8) % 16
            back_send[d, :, part(g), :] = owned((k + d) % 16, g)
            bs_copy(g, d).start()
            return carry

        lax.fori_loop(0, 8, give, 0)
        lax.fori_loop(9, 16, give, 0)
        back_rows[g][pl.ds(pl.multiple_of(8 * k, 8), 8), part(g), :] = owned(k, g)

    def bx_copy(g, d):
        return push(
            back_pick.at[d, :, part(g), :], back_in_x.at[x, :, part(g), :],
            bx_send.at[g, d], bx_recv.at[g, d], at_x((x + d) % 4),
        )

    for g in range(PARTS):

        def given(d, carry):
            landed(
                back_rows[g].at[
                    pl.ds(pl.multiple_of(8 * ((k + 16 - d) % 16), 8), 8), part(g), :
                ],
                bs_recv.at[g, d],
            )
            return carry

        lax.fori_loop(1, 16, given, 0)
        for d in (2, 1, 3, 0):
            other = (x + d) % 4

            def turned(n, carry):
                for r in range(8):
                    i = 8 * n + r
                    back_pick[d, i, part(g), :] = back_rows[g][
                        (32 * other + i + 128 - first) & 127, part(g), :
                    ]
                return carry

            lax.fori_loop(0, 4, turned, 0)
            if d:
                bx_copy(g, d).start()
            else:
                back_in_x[x, :, part(g), :] = back_pick[0, :, part(g), :]

    def by_copy(g, d):
        return push(
            back_sum.at[d, :, part(g), :], back_in_y.at[d, :, part(g), :],
            by_send.at[g, d], by_recv.at[g, d], at_y((yl + d) % 4),
        )

    for g in range(PARTS):
        for d in (1, 3, 2):
            landed(back_in_x.at[(x + 4 - d) % 4, :, part(g), :], bx_recv.at[g, d])
        for d in (2, 1, 3, 0):
            total = jnp.zeros((32, WIDE, 128), F32)
            for other in range(4):
                total += jnp.where(
                    super_of(other, g) == (yl + d) % 4, back_in_x[other, :, part(g), :], 0.0
                )
            back_sum[d, :, part(g), :] = total
            if d:
                by_copy(g, d).start()
    for g in range(PARTS):
        for d in (1, 2, 3):
            landed(back_in_y.at[d, :, part(g), :], by_recv.at[g, d])
    out[...] = back_sum[0] + back_in_y[1] + back_in_y[2] + back_in_y[3]

    for d in (1, 2, 3):
        a_copy(d).wait_send()
    for g in range(PARTS):
        for d in (1, 2, 3):
            y_copy(g, d).wait_send()
            x_copy(g, d).wait_send()
            bx_copy(g, d).wait_send()
            by_copy(g, d).wait_send()

        def left(d, carry):
            s_copy(g, d).wait_send()
            bs_copy(g, d).wait_send()
            return carry

        lax.fori_loop(1, 16, left, 0)
        h_copy(g).wait_send()
        bh_copy(g).wait_send()
    for n in range(5):
        halo_done(n)
    for n in range(4):
        for h in range(2):

            @pl.when(jnp.logical_not(stays(h)))
            def _():
                field_copy(n, h).wait_send()


def on_device(
    courant, anchor, source, wavelet, receivers, observed,
    wave_before, wave_now, adjoint_after, adjoint_now,
):
    vmem, smem = pltpu.VMEM, pltpu.SMEM
    dma = pltpu.SemaphoreType.DMA
    return pl.pallas_call(
        kernel,
        out_shape=jax.ShapeDtypeStruct((32, 8, 128), F32),
        in_specs=[pl.BlockSpec(memory_space=pltpu.HBM)] * 10,
        out_specs=pl.BlockSpec(memory_space=vmem),
        scratch_shapes=[
            vmem((4, 32, 8, 128), F32),
            vmem((4, 32, 8, 128), F32),
            vmem((128, 8, 128), F32),
            vmem((128, 8, 128), F32),
            vmem((16, 8, 8, 128), F32),
            vmem((16, 8, 8, 128), F32),
            vmem((16, 8, 8, 128), F32),
            vmem((2, 2, 8, 8, 128), F32),
            vmem((2, 2, 2, 8, 8, 128), F32),
            vmem((8, 128, 128), F32),
            vmem((8, 64, 128), F32),
            vmem((5, 16, 80, 128), F32),
            vmem((8, 64, 128), F32),
            vmem((8, 64, 128), F32),
            vmem((8, 64, 128), F32),
            vmem((3, 8, 64, 128), F32),
            vmem((8, 64, 128), F32),
            vmem((2, 8, 64, 128), F32),
            vmem((8, 64, 128), F32),
            vmem((8, 128, 128), F32),
            vmem((2, 2, 2, 8, 8, 128), F32),
            vmem((2, 2, 8, 8, 128), F32),
            vmem((16, 8, 8, 128), F32),
            vmem((128, 8, 128), F32),
            vmem((128, 8, 128), F32),
            vmem((4, 32, 8, 128), F32),
            vmem((4, 32, 8, 128), F32),
            vmem((4, 32, 8, 128), F32),
            vmem((4, 32, 8, 128), F32),
            vmem((4, 8, 128), I32),
            vmem((8, 128), I32),
            smem((1, 2), I32),
            smem((1, 3), I32),
            smem((1, 3), F32),
            vmem((3, 1, 64), I32),
            vmem((3, 1, 64), F32),
            vmem((128, 128), F32),
            vmem((64, 512), F32),
            vmem((64, 128), F32),
            vmem((3, 64, 1), F32),
            dma((6,)),
            dma((4, 2)), dma((4, 2)),
            dma((PARTS, 4)), dma((PARTS, 4)),
            dma((4,)), dma((4,)),
            dma((PARTS, 4)), dma((PARTS, 4)),
            dma((PARTS, 16)), dma((PARTS, 16)),
            dma((PARTS,)), dma((PARTS,)),
            dma((5, 3)), dma((5, 3)),
            dma((PARTS,)), dma((PARTS,)),
            dma((PARTS, 16)), dma((PARTS, 16)),
            dma((PARTS, 4)), dma((PARTS, 4)),
            dma((PARTS, 4)), dma((PARTS, 4)),
        ],
        compiler_params=pltpu.CompilerParams(
            collective_id=0, has_side_effects=True, vmem_limit_bytes=60 * 1024 * 1024
        ),
    )(
        anchor, source, wavelet, receivers.transpose(2, 0, 1), observed.transpose(1, 0, 2), courant,
        wave_before, wave_now, adjoint_after, adjoint_now,
    )


def solution(mesh):
    return jax.shard_map(
        on_device,
        mesh=mesh,
        in_specs=(
            P("shot", "space", None),
            P("shot", None),
            P("shot", None),
            P("shot", None),
            P("shot", None, None),
            P("shot", None, None),
            P("shot", "space", None, None),
            P("shot", "space", None, None),
            P("shot", "space", None, None),
            P("shot", "space", None, None),
        ),
        out_specs=P("shot", "space", None),
        check_vma=False,
    )
```

```python
import jax
import jax.numpy as jnp
from jax import lax
from jax.experimental import pallas as pl
from jax.experimental.pallas import tpu as pltpu
from jax.sharding import PartitionSpec as P

MESH = pl.DeviceIdType.MESH
HIGH = lax.Precision.HIGHEST
COEF = (-205.0 / 72.0, 8.0 / 5.0, -1.0 / 5.0, 8.0 / 315.0, -1.0 / 560.0)
F32 = jnp.float32
I32 = jnp.int32
PARTS = 2
WIDE = 8 // PARTS


def kernel(
    anchor_in, source_in, wavelet_in, receivers_in, observed_in, courant, wave_before, wave_now,
    adjoint_after, adjoint_now, out,
    gath, picked, rows_0, rows_1, rowsend, cols_0, cols_1, halfsend, half, twice, speed,
    pad, ends, sides, before, after_now, after, laps, third, adj, spot, images,
    back_half, back_in, back_send, back_rows_0, back_rows_1, back_pick, back_in_x, back_sum, back_in_y,
    anchors, anchor_own, anchor, source, wavelet, receivers, observed, band, hits, deeps, seens,
    local_sem, field_send, field_recv, y_send, y_recv, a_send, a_recv, x_send, x_recv,
    s_send, s_recv, h_send, h_recv, halo_send, halo_recv,
    bh_send, bh_recv, bs_send, bs_recv, bx_send, bx_recv, by_send, by_recv,
):
    rows, cols, back_rows = (rows_0, rows_1), (cols_0, cols_1), (back_rows_0, back_rows_1)
    shot = lax.axis_index("shot")
    space = lax.axis_index("space")
    yl, x = shot // 4, shot % 4
    z, yh, c = space // 4, (space // 2) % 2, space % 2
    k = 2 * z + c

    def at_k(other):
        return (shot, (other // 2) * 4 + yh * 2 + other % 2)

    def at_x(other):
        return (yl * 4 + other, space)

    def at_y(other):
        return (other * 4 + x, space)

    partner = (shot, z * 4 + (1 - yh) * 2 + c)
    diagonal = (shot, z * 4 + (1 - yh) * 2 + (1 - c))

    def push(src, dst, send, recv, device):
        return pltpu.make_async_remote_copy(
            src_ref=src, dst_ref=dst, send_sem=send, recv_sem=recv,
            device_id=device, device_id_type=MESH,
        )

    def landed(dst, sem):
        pltpu.make_async_copy(dst, dst, sem).wait()

    barrier = pltpu.get_barrier_semaphore()
    for d in range(1, 4):
        pl.semaphore_signal(barrier, 1, device_id=at_x((x + d) % 4), device_id_type=MESH)
        pl.semaphore_signal(barrier, 1, device_id=at_y((yl + d) % 4), device_id_type=MESH)
    for d in range(1, 16):
        pl.semaphore_signal(barrier, 1, device_id=at_k((k + d) % 16), device_id_type=MESH)
    pl.semaphore_signal(barrier, 1, device_id=partner, device_id_type=MESH)
    pl.semaphore_signal(barrier, 1, device_id=diagonal, device_id_type=MESH)
    small = [
        pltpu.make_async_copy(src, dst, local_sem.at[1 + n])
        for n, (src, dst) in enumerate(
            (
                (anchor_in, anchor), (source_in, source), (wavelet_in, wavelet),
                (receivers_in, receivers), (observed_in, observed),
            )
        )
    ]
    for copy in small:
        copy.start()

    for copy in small:
        copy.wait()
    ox, oy = anchor[0, 0], anchor[0, 1]
    anchor_own[...] = jnp.full((8, 128), ox, I32)
    anchors[x] = jnp.full((8, 128), ox, I32)


    pl.semaphore_wait(barrier, 23)

    def part(g):
        return pl.ds(WIDE * g, WIDE)

    def y_copy(g, d):
        return push(
            courant.at[:, part(g), :], gath.at[yl, :, part(g), :],
            y_send.at[g, d], y_recv.at[g, d], at_y((yl + d) % 4),
        )

    own_model = pltpu.make_async_copy(courant, gath.at[yl], local_sem.at[0])
    own_model.start()

    def a_copy(d):
        return push(anchor_own, anchors.at[x], a_send.at[d], a_recv.at[d], at_x((x + d) % 4))

    for d in (1, 2, 3):
        a_copy(d).start()
    for g in range(PARTS):
        for d in (2, 1, 3):
            y_copy(g, d).start()

    def field_parts(n):
        src = (wave_now, wave_before, adjoint_now, adjoint_after)[n]

        def dst(core):
            if n == 0:
                return pad.at[0, pl.ds(4 + 4 * core, 4), pl.ds(8, 64)]
            return (before, after_now, after)[n - 1].at[pl.ds(4 * core, 4)]

        return src, dst

    def field_copy(n, h):
        src, dst = field_parts(n)
        return push(
            src.at[0, :, pl.ds(64 * h, 64), :], dst(c), field_send.at[n, h], field_recv.at[n, c],
            (shot, z * 4 + 2 * h + yh),
        )

    def stays(h):
        return jnp.logical_and(yh == h, c == h)

    def field_start(n):
        src, dst = field_parts(n)
        for h in range(2):

            @pl.when(stays(h))
            def _():
                pltpu.make_async_copy(
                    src.at[0, :, pl.ds(64 * h, 64), :], dst(c), field_recv.at[n, c]
                ).start()

            @pl.when(jnp.logical_not(stays(h)))
            def _():
                field_copy(n, h).start()

    def field_wait(n):
        src, dst = field_parts(n)
        for core in range(2):
            landed(dst(core), field_recv.at[n, core])

    for n in range(5):
        pad[n, 0:4] = jnp.zeros((4, 80, 128), F32)
        pad[n, 12:16] = jnp.zeros((4, 80, 128), F32)
        pad[n, 4:12, 0:8] = jnp.zeros((8, 8, 128), F32)
        pad[n, 4:12, 72:80] = jnp.zeros((8, 8, 128), F32)
        sides[n, :, 8:16] = jnp.zeros((8, 8, 128), F32)

    @pl.when(yh == 0)
    def _():
        for n in range(5):
            sides[n, :, 4:8] = jnp.zeros((8, 4, 128), F32)

    @pl.when(yh == 1)
    def _():
        for n in range(5):
            sides[n, :, 16:20] = jnp.zeros((8, 4, 128), F32)

    for side, first_or_last in ((0, 0), (1, 15)):

        @pl.when(k == first_or_last)
        def _():
            for n in range(5):
                ends[n, side] = jnp.zeros((4, 64, 128), F32)

    square = lax.broadcasted_iota(I32, (64, 64), 0) == lax.broadcasted_iota(I32, (64, 64), 1)

    def upright(row):
        return jnp.sum(
            jnp.where(square, jnp.broadcast_to(row.astype(F32), (64, 64)), 0.0),
            axis=1, keepdims=True,
        )

    row_of = receivers[0] - 8 * k
    col_of = receivers[1] - 64 * yh
    inside = (row_of >= 0) & (row_of < 8) & (col_of >= 0) & (col_of < 64)
    flat = upright(jnp.where(inside, row_of * 64 + col_of, -1))
    hits[...] = jnp.where(
        lax.broadcasted_iota(I32, (64, 512), 1).astype(F32) == flat, 1.0, 0.0
    ).astype(F32)
    deeps[...] = jnp.where(
        lax.broadcasted_iota(I32, (64, 128), 1).astype(F32) == upright(receivers[2]), 1.0, 0.0
    ).astype(F32)
    for n in range(3):
        seens[n] = upright(observed[n])
    apart = jnp.abs(
        lax.broadcasted_iota(I32, (128, 128), 0) - lax.broadcasted_iota(I32, (128, 128), 1)
    )
    line = jnp.where(apart == 0, 3.0 * COEF[0], 0.0)
    for reach in range(1, 5):
        line = jnp.where(apart == reach, COEF[reach], line)
    band[...] = line.astype(F32)
    s_row, s_col, s_dep = source[0, 0] - 8 * k, source[0, 1] - 64 * yh, source[0, 2]
    spot[...] = jnp.where(
        (lax.broadcasted_iota(I32, (8, 64, 128), 0) == s_row)
        & (lax.broadcasted_iota(I32, (8, 64, 128), 1) == s_col)
        & (lax.broadcasted_iota(I32, (8, 64, 128), 2) == s_dep),
        1.0, 0.0,
    ).astype(F32)

    def record(field, n):
        lines = jnp.dot(
            hits[...], field.reshape(512, 128), precision=HIGH, preferred_element_type=F32
        )
        return jnp.sum(lines * deeps[...], axis=1, keepdims=True) - seens[n]

    def inject(residual):
        return lax.dot_general(
            hits[...], deeps[...] * residual, (((0,), (0,)), ((), ())),
            precision=HIGH, preferred_element_type=F32,
        ).reshape(8, 64, 128)

    def end_copy(n, way):
        return push(
            pad.at[n, pl.ds(4 + 4 * way, 4), pl.ds(8, 64)], ends.at[n, 1 - way],
            halo_send.at[n, way], halo_recv.at[n, way], at_k((k + 15 + 2 * way) % 16),
        )

    def side_copy(n, half_of):
        return push(
            pad.at[n, pl.ds(4, 8), pl.ds(68 - 60 * half_of, 4)],
            sides.at[n, :, pl.ds(4 + 12 * half_of, 4)],
            halo_send.at[n, 2], halo_recv.at[n, 2], partner,
        )

    def end_there(way):
        return k > 0 if way == 0 else k < 15

    def end_start(n, way):
        @pl.when(end_there(way))
        def _():
            end_copy(n, way).start()

    def side_start(n):
        for half_of in range(2):

            @pl.when(yh == half_of)
            def _():
                side_copy(n, half_of).start()

    def halo_start(n):
        side_start(n)
        for way in range(2):
            end_start(n, way)

    def halo_wait(n):
        for way in range(2):

            @pl.when(end_there(1 - way))
            def _():
                landed(ends.at[n, 1 - way], halo_recv.at[n, way])

        for half_of in range(2):

            @pl.when(yh != half_of)
            def _():
                landed(sides.at[n, :, pl.ds(4 + 12 * half_of, 4)], halo_recv.at[n, 2])

    def halo_done(n):
        for way in range(2):

            @pl.when(end_there(way))
            def _():
                end_copy(n, way).wait_send()

        for half_of in range(2):

            @pl.when(yh == half_of)
            def _():
                side_copy(n, half_of).wait_send()

    def close(n, lap, new, weight, send):
        def add(row, at, wide, extra):
            if lap is not None:
                lap[row, pl.ds(at, wide)] = lap[row, pl.ds(at, wide)] + extra
            below, right = (4, 8) if send else (0, 0)
            place = pl.ds(pl.multiple_of(right + at, 8), wide)
            new[below + row, place] = new[below + row, place] + weight[row, pl.ds(at, wide)] * extra

        def from_end(way, i, at, wide):
            total = None
            for d in range(i + 1, 5):
                row = 4 + i - d if way == 0 else d - i - 1
                term = COEF[d] * ends[n, way, row, pl.ds(at, wide)]
                total = term if total is None else total + term
            return total

        beside = None
        for d in range(1, 5):
            term = COEF[d] * (sides[n, :, 8 - d : 16 - d] + sides[n, :, 8 + d : 16 + d])
            beside = term if beside is None else beside + term
        edge = pl.multiple_of(56 - 56 * yh, 8)
        rest = pl.multiple_of(8 * yh, 8)
        for way in range(2):
            for i in range(4):
                row = i if way == 0 else 7 - i
                add(row, edge, 8, beside[row] + from_end(way, i, edge, 8))
        if send:
            side_start(n + 1)

        def rows_of(way):
            for i in range(4):
                row = i if way == 0 else 7 - i
                add(row, rest, 56, from_end(way, i, rest, 56))
            if send:
                end_start(n + 1, way)

        @pl.when(c == 0)
        def _():
            rows_of(0)
            rows_of(1)

        @pl.when(c == 1)
        def _():
            rows_of(1)
            rows_of(0)

    def laplace(n):
        total = jnp.dot(
            pad[n, 4:12, 8:72].reshape(512, 128), band[...],
            precision=HIGH, preferred_element_type=F32,
        ).reshape(8, 64, 128)
        for d in range(1, 5):
            beside = pad[n, 4 - d : 12 - d, 8:72] + pad[n, 4 + d : 12 + d, 8:72]
            beside += pad[n, 4:12, 8 - d : 72 - d] + pad[n, 4:12, 8 + d : 72 + d]
            total += COEF[d] * beside
        return total

    own_model.wait()
    for d in (1, 2, 3):
        landed(anchors.at[(x + 4 - d) % 4], a_recv.at[d])

    def super_of(other, g):
        start = anchors[other, part(g), :]
        residue = 32 * x + lax.broadcasted_iota(I32, (32, WIDE, 128), 0)
        return (start >> 7)[None] + jnp.where(residue < (start & 127)[None], 1, 0)

    def x_copy(g, d):
        return push(
            picked.at[d, :, part(g), :],
            rows[g].at[pl.ds(pl.multiple_of(32 * x, 32), 32), part(g), :],
            x_send.at[g, d], x_recv.at[g, d], at_x((x + d) % 4),
        )

    for g in range(PARTS):
        for d in (1, 3, 2):
            landed(gath.at[(yl + 4 - d) % 4, :, part(g), :], y_recv.at[g, d])
        for d in (2, 1, 3, 0):
            which = super_of((x + d) % 4, g)
            chosen = gath[0, :, part(g), :]
            for q in range(1, 4):
                chosen = jnp.where(which == q, gath[q, :, part(g), :], chosen)
            if d:
                picked[d, :, part(g), :] = chosen
                x_copy(g, d).start()
            else:
                rows[g][pl.ds(pl.multiple_of(32 * x, 32), 32), part(g), :] = chosen
    field_start(0)
    field_start(1)

    first = ox & 127

    def s_copy(g, d):
        return push(
            rowsend.at[d, :, part(g), :], cols[g].at[k, :, part(g), :],
            s_send.at[g, d], s_recv.at[g, d], at_k((k + d) % 16),
        )

    for g in range(PARTS):
        for d in (1, 3, 2):
            landed(
                rows[g].at[pl.ds(pl.multiple_of(32 * ((x + 4 - d) % 4), 32), 32), part(g), :],
                x_recv.at[g, d],
            )

        def spread(n, carry):
            d = (n + 8) % 16
            other = (k + d) % 16
            for r in range(8):
                rowsend[d, r, part(g), :] = rows[g][(first + 8 * other + r) & 127, part(g), :]
            s_copy(g, d).start()
            return carry

        lax.fori_loop(0, 8, spread, 0)
        lax.fori_loop(9, 16, spread, 0)
        for r in range(8):
            cols[g][k, r, part(g), :] = rows[g][(first + 8 * k + r) & 127, part(g), :]

    turn = oy & 63

    def columns(h, e, core, g):
        at = (oy >> 6) + h
        place = 32 * e + 16 * yh + 8 * core + WIDE * g + lax.broadcasted_iota(I32, (8, WIDE, 128), 1)
        low = cols[g][4 * at + 2 * e + core, :, part(g), :]
        high = cols[g][4 * jnp.minimum(at + 1, 3) + 2 * e + core, :, part(g), :]
        return jnp.where(place < turn, high, low)

    def h_copy(g):
        return push(
            halfsend.at[:, :, :, part(g), :], half.at[yh, :, :, :, part(g), :],
            h_send.at[g], h_recv.at[g], partner,
        )

    for g in range(PARTS):

        def spread_in(d, carry):
            landed(cols[g].at[(k + 16 - d) % 16, :, part(g), :], s_recv.at[g, d])
            return carry

        lax.fori_loop(1, 16, spread_in, 0)
        for e in range(2):
            for core in range(2):
                halfsend[e, core, :, part(g), :] = columns(1 - yh, e, core, g)
        h_copy(g).start()
        for e in range(2):
            for core in range(2):
                half[yh, e, core, :, part(g), :] = columns(yh, e, core, g)
        if g == 0:
            field_wait(0)
            halo_start(0)
    field_start(2)
    field_start(3)
    laps[0] = laplace(0)
    field_wait(1)
    pad[1, 4:12, 8:72] = 2.0 * pad[0, 4:12, 8:72] - before[...] + wavelet[0, 0] * spot[...]
    third[...] = jnp.zeros((8, 64, 128), F32)
    halo_wait(0)
    close(0, laps.at[0], third, spot, False)
    for g in range(PARTS):
        landed(half.at[1 - yh, :, :, :, part(g), :], h_recv.at[g])
    for e in range(2):
        for b in range(2):
            for core in range(2):
                t = 4 * e + 2 * b + core
                twice[:, 8 * t : 8 * t + 8] = half[b, e, core]
                twice[:, 64 + 8 * t : 72 + 8 * t] = half[b, e, core]
    for r in range(8):
        speed[r] = twice[r, pl.ds(turn, 64)]

    pad[1, 4:12, 8:72] = pad[1, 4:12, 8:72] + speed[...] * laps[0]
    halo_start(1)
    laps[1] = laplace(1)
    pad[2, 4:12, 8:72] = (
        2.0 * pad[1, 4:12, 8:72] - pad[0, 4:12, 8:72] + wavelet[0, 1] * spot[...]
        + speed[...] * laps[1]
    )
    residual0 = record(pad[1, 4:12, 8:72], 0)
    halo_wait(1)
    close(1, laps.at[1], pad.at[2], speed, True)
    laps[2] = laplace(2)
    third[...] = (
        2.0 * pad[2, 4:12, 8:72] - pad[1, 4:12, 8:72] + wavelet[0, 2] * spot[...]
        + speed[...] * laps[2]
    )
    residual1 = record(pad[2, 4:12, 8:72], 1)
    halo_wait(2)
    close(2, laps.at[2], third, speed, False)
    residual2 = record(third[...], 2)

    field_wait(2)
    adj[0] = after_now[...] + inject(residual2)
    pad[3, 4:12, 8:72] = speed[...] * adj[0]
    halo_start(3)
    field_wait(3)
    adj[1] = 2.0 * adj[0] - after[...] + inject(residual1) + laplace(3)
    pad[4, 4:12, 8:72] = speed[...] * adj[1]
    images[:, 0:64] = adj[0] * laps[2]
    halo_wait(3)
    close(3, adj.at[1], pad.at[4], speed, True)
    third[...] = 2.0 * adj[1] - adj[0] + inject(residual0) + laplace(4)
    images[:, 0:64] = images[:, 0:64] + adj[1] * laps[1] + third[...] * laps[0]
    halo_wait(4)
    close(4, None, images, laps.at[0], False)
    images[:, 64:128] = images[:, 0:64]

    for r in range(8):
        line = images[r, pl.ds(64 - turn, 64)]
        for e in range(2):
            for b in range(2):
                for core in range(2):
                    t = 4 * e + 2 * b + core
                    back_half[b, e, core, r] = line[8 * t : 8 * t + 8]

    def bh_copy(g):
        return push(
            back_half.at[1 - yh, :, :, :, part(g), :], back_in.at[:, :, :, part(g), :],
            bh_send.at[g], bh_recv.at[g], partner,
        )

    for g in range(PARTS):
        bh_copy(g).start()

    def owned(other, g):
        zz, core = other // 2, other % 2
        e, q = zz % 2, zz // 2
        place = 32 * e + 16 * yh + 8 * core + WIDE * g + lax.broadcasted_iota(I32, (WIDE, 128), 0)
        wraps = jnp.where(place < turn, 1, 0)
        mine = (wraps + ((oy >> 6) + yh) == q)[None]
        theirs = (wraps + ((oy >> 6) + 1 - yh) == q)[None]
        return jnp.where(mine, back_half[yh, e, core, :, part(g), :], 0.0) + jnp.where(
            theirs, back_in[e, core, :, part(g), :], 0.0
        )

    def bs_copy(g, d):
        return push(
            back_send.at[d, :, part(g), :],
            back_rows[g].at[pl.ds(pl.multiple_of(8 * k, 8), 8), part(g), :],
            bs_send.at[g, d], bs_recv.at[g, d], at_k((k + d) % 16),
        )

    for g in range(PARTS):
        landed(back_in.at[:, :, :, part(g), :], bh_recv.at[g])

        def give(n, carry):
            d = (n + 8) % 16
            back_send[d, :, part(g), :] = owned((k + d) % 16, g)
            bs_copy(g, d).start()
            return carry

        lax.fori_loop(0, 8, give, 0)
        lax.fori_loop(9, 16, give, 0)
        back_rows[g][pl.ds(pl.multiple_of(8 * k, 8), 8), part(g), :] = owned(k, g)

    def bx_copy(g, d):
        return push(
            back_pick.at[d, :, part(g), :], back_in_x.at[x, :, part(g), :],
            bx_send.at[g, d], bx_recv.at[g, d], at_x((x + d) % 4),
        )

    for g in range(PARTS):

        def given(d, carry):
            landed(
                back_rows[g].at[
                    pl.ds(pl.multiple_of(8 * ((k + 16 - d) % 16), 8), 8), part(g), :
                ],
                bs_recv.at[g, d],
            )
            return carry

        lax.fori_loop(1, 16, given, 0)
        for d in (2, 1, 3, 0):
            other = (x + d) % 4

            def turned(n, carry):
                for r in range(8):
                    i = 8 * n + r
                    back_pick[d, i, part(g), :] = back_rows[g][
                        (32 * other + i + 128 - first) & 127, part(g), :
                    ]
                return carry

            lax.fori_loop(0, 4, turned, 0)
            if d:
                bx_copy(g, d).start()
            else:
                back_in_x[x, :, part(g), :] = back_pick[0, :, part(g), :]

    def by_copy(g, d):
        return push(
            back_sum.at[d, :, part(g), :], back_in_y.at[d, :, part(g), :],
            by_send.at[g, d], by_recv.at[g, d], at_y((yl + d) % 4),
        )

    for g in range(PARTS):
        for d in (1, 3, 2):
            landed(back_in_x.at[(x + 4 - d) % 4, :, part(g), :], bx_recv.at[g, d])
        for d in (2, 1, 3, 0):
            total = jnp.zeros((32, WIDE, 128), F32)
            for other in range(4):
                total += jnp.where(
                    super_of(other, g) == (yl + d) % 4, back_in_x[other, :, part(g), :], 0.0
                )
            back_sum[d, :, part(g), :] = total
            if d:
                by_copy(g, d).start()
    for g in range(PARTS):
        for d in (1, 2, 3):
            landed(back_in_y.at[d, :, part(g), :], by_recv.at[g, d])
    out[...] = back_sum[0] + back_in_y[1] + back_in_y[2] + back_in_y[3]

    for d in (1, 2, 3):
        a_copy(d).wait_send()
    for g in range(PARTS):
        for d in (1, 2, 3):
            y_copy(g, d).wait_send()
            x_copy(g, d).wait_send()
            bx_copy(g, d).wait_send()
            by_copy(g, d).wait_send()

        def left(d, carry):
            s_copy(g, d).wait_send()
            bs_copy(g, d).wait_send()
            return carry

        lax.fori_loop(1, 16, left, 0)
        h_copy(g).wait_send()
        bh_copy(g).wait_send()
    for n in range(5):
        halo_done(n)
    for n in range(4):
        for h in range(2):

            @pl.when(jnp.logical_not(stays(h)))
            def _():
                field_copy(n, h).wait_send()


def on_device(
    courant, anchor, source, wavelet, receivers, observed,
    wave_before, wave_now, adjoint_after, adjoint_now,
):
    vmem, smem = pltpu.VMEM, pltpu.SMEM
    dma = pltpu.SemaphoreType.DMA
    return pl.pallas_call(
        kernel,
        out_shape=jax.ShapeDtypeStruct((32, 8, 128), F32),
        in_specs=[pl.BlockSpec(memory_space=pltpu.HBM)] * 10,
        out_specs=pl.BlockSpec(memory_space=vmem),
        scratch_shapes=[
            vmem((4, 32, 8, 128), F32),
            vmem((4, 32, 8, 128), F32),
            vmem((128, 8, 128), F32),
            vmem((128, 8, 128), F32),
            vmem((16, 8, 8, 128), F32),
            vmem((16, 8, 8, 128), F32),
            vmem((16, 8, 8, 128), F32),
            vmem((2, 2, 8, 8, 128), F32),
            vmem((2, 2, 2, 8, 8, 128), F32),
            vmem((8, 128, 128), F32),
            vmem((8, 64, 128), F32),
            vmem((5, 16, 80, 128), F32),
            vmem((5, 2, 4, 64, 128), F32),
            vmem((5, 8, 24, 128), F32),
            vmem((8, 64, 128), F32),
            vmem((8, 64, 128), F32),
            vmem((8, 64, 128), F32),
            vmem((3, 8, 64, 128), F32),
            vmem((8, 64, 128), F32),
            vmem((2, 8, 64, 128), F32),
            vmem((8, 64, 128), F32),
            vmem((8, 128, 128), F32),
            vmem((2, 2, 2, 8, 8, 128), F32),
            vmem((2, 2, 8, 8, 128), F32),
            vmem((16, 8, 8, 128), F32),
            vmem((128, 8, 128), F32),
            vmem((128, 8, 128), F32),
            vmem((4, 32, 8, 128), F32),
            vmem((4, 32, 8, 128), F32),
            vmem((4, 32, 8, 128), F32),
            vmem((4, 32, 8, 128), F32),
            vmem((4, 8, 128), I32),
            vmem((8, 128), I32),
            smem((1, 2), I32),
            smem((1, 3), I32),
            smem((1, 3), F32),
            vmem((3, 1, 64), I32),
            vmem((3, 1, 64), F32),
            vmem((128, 128), F32),
            vmem((64, 512), F32),
            vmem((64, 128), F32),
            vmem((3, 64, 1), F32),
            dma((6,)),
            dma((4, 2)), dma((4, 2)),
            dma((PARTS, 4)), dma((PARTS, 4)),
            dma((4,)), dma((4,)),
            dma((PARTS, 4)), dma((PARTS, 4)),
            dma((PARTS, 16)), dma((PARTS, 16)),
            dma((PARTS,)), dma((PARTS,)),
            dma((5, 3)), dma((5, 3)),
            dma((PARTS,)), dma((PARTS,)),
            dma((PARTS, 16)), dma((PARTS, 16)),
            dma((PARTS, 4)), dma((PARTS, 4)),
            dma((PARTS, 4)), dma((PARTS, 4)),
        ],
        compiler_params=pltpu.CompilerParams(
            collective_id=0, has_side_effects=True, vmem_limit_bytes=60 * 1024 * 1024
        ),
    )(
        anchor, source, wavelet, receivers.transpose(2, 0, 1), observed.transpose(1, 0, 2), courant,
        wave_before, wave_now, adjoint_after, adjoint_now,
    )


def solution(mesh):
    return jax.shard_map(
        on_device,
        mesh=mesh,
        in_specs=(
            P("shot", "space", None),
            P("shot", None),
            P("shot", None),
            P("shot", None),
            P("shot", None, None),
            P("shot", None, None),
            P("shot", "space", None, None),
            P("shot", "space", None, None),
            P("shot", "space", None, None),
            P("shot", "space", None, None),
        ),
        out_specs=P("shot", "space", None),
        check_vma=False,
    )
```

```python
import jax
import jax.numpy as jnp
from jax import lax
from jax.experimental import pallas as pl
from jax.experimental.pallas import tpu as pltpu
from jax.sharding import PartitionSpec as P

MESH = pl.DeviceIdType.MESH
HIGH = lax.Precision.HIGHEST
COEF = (-205.0 / 72.0, 8.0 / 5.0, -1.0 / 5.0, 8.0 / 315.0, -1.0 / 560.0)
F32 = jnp.float32
I32 = jnp.int32
PARTS = 2
WIDE = 8 // PARTS


def kernel(
    anchor_in, source_in, wavelet_in, receivers_in, observed_in, courant, wave_before, wave_now,
    adjoint_after, adjoint_now, out,
    gath, picked, rows_0, rows_1, rowsend, cols_0, cols_1, halfsend, half, twice, speed,
    pad, ends, sides, before, after_now, after, laps, third, adj, spot, images,
    back_half, back_in, back_send, back_rows_0, back_rows_1, back_pick, back_in_x, back_sum, back_in_y,
    anchors, anchor_own, anchor, source, wavelet, receivers, observed, band, hits, deeps, seens,
    local_sem, field_send, field_recv, y_send, y_recv, a_send, a_recv, x_send, x_recv,
    s_send, s_recv, h_send, h_recv, halo_send, halo_recv,
    bh_send, bh_recv, bs_send, bs_recv, bx_send, bx_recv, by_send, by_recv, relay_send,
):
    rows, cols, back_rows = (rows_0, rows_1), (cols_0, cols_1), (back_rows_0, back_rows_1)
    shot = lax.axis_index("shot")
    space = lax.axis_index("space")
    yl, x = shot // 4, shot % 4
    z, yh, c = space // 4, (space // 2) % 2, space % 2
    k = 2 * z + c

    def at_k(other):
        return (shot, (other // 2) * 4 + yh * 2 + other % 2)

    def at_x(other):
        return (yl * 4 + other, space)

    def at_y(other):
        return (other * 4 + x, space)

    partner = (shot, z * 4 + (1 - yh) * 2 + c)
    diagonal = (shot, z * 4 + (1 - yh) * 2 + (1 - c))

    def push(src, dst, send, recv, device):
        return pltpu.make_async_remote_copy(
            src_ref=src, dst_ref=dst, send_sem=send, recv_sem=recv,
            device_id=device, device_id_type=MESH,
        )

    def landed(dst, sem):
        pltpu.make_async_copy(dst, dst, sem).wait()

    barrier = pltpu.get_barrier_semaphore()
    for d in range(1, 4):
        pl.semaphore_signal(barrier, 1, device_id=at_x((x + d) % 4), device_id_type=MESH)
        pl.semaphore_signal(barrier, 1, device_id=at_y((yl + d) % 4), device_id_type=MESH)
    for d in range(1, 16):
        pl.semaphore_signal(barrier, 1, device_id=at_k((k + d) % 16), device_id_type=MESH)
    pl.semaphore_signal(barrier, 1, device_id=partner, device_id_type=MESH)
    pl.semaphore_signal(barrier, 1, device_id=diagonal, device_id_type=MESH)
    small = [
        pltpu.make_async_copy(src, dst, local_sem.at[1 + n])
        for n, (src, dst) in enumerate(
            (
                (anchor_in, anchor), (source_in, source), (wavelet_in, wavelet),
                (receivers_in, receivers), (observed_in, observed),
            )
        )
    ]
    for copy in small:
        copy.start()

    for copy in small:
        copy.wait()
    ox, oy = anchor[0, 0], anchor[0, 1]
    anchor_own[...] = jnp.full((8, 128), ox, I32)
    anchors[x] = jnp.full((8, 128), ox, I32)


    pl.semaphore_wait(barrier, 23)

    def part(g):
        return pl.ds(WIDE * g, WIDE)

    def y_copy(g, d):
        return push(
            courant.at[:, part(g), :], gath.at[yl, :, part(g), :],
            y_send.at[g, d], y_recv.at[g, d], at_y((yl + d) % 4),
        )

    own_model = pltpu.make_async_copy(courant, gath.at[yl], local_sem.at[0])
    own_model.start()

    def y_direct(d):
        if d == 2:
            return yl >= 0
        return yl != (0 if d == 3 else 3)

    inner = jnp.logical_and(yl > 0, yl < 3)

    def y_relay(g):
        slot = gath.at[(yl + 2) % 4, :, part(g), :]
        return push(slot, slot, relay_send.at[g], y_recv.at[g, 2 * yl - 1], at_y(3 * (yl - 1)))

    def a_copy(d):
        return push(anchor_own, anchors.at[x], a_send.at[d], a_recv.at[d], at_x((x + d) % 4))

    for d in (1, 2, 3):
        a_copy(d).start()
    for g in range(PARTS):
        for d in (2, 1, 3):

            @pl.when(y_direct(d))
            def _():
                y_copy(g, d).start()

    def field_parts(n):
        src = (wave_now, wave_before, adjoint_now, adjoint_after)[n]

        def dst(core):
            if n == 0:
                return pad.at[0, pl.ds(4 + 4 * core, 4), pl.ds(8, 64)]
            return (before, after_now, after)[n - 1].at[pl.ds(4 * core, 4)]

        return src, dst

    def field_copy(n, h):
        src, dst = field_parts(n)
        return push(
            src.at[0, :, pl.ds(64 * h, 64), :], dst(c), field_send.at[n, h], field_recv.at[n, c],
            (shot, z * 4 + 2 * h + yh),
        )

    def stays(h):
        return jnp.logical_and(yh == h, c == h)

    def field_start(n):
        src, dst = field_parts(n)
        for h in range(2):

            @pl.when(stays(h))
            def _():
                pltpu.make_async_copy(
                    src.at[0, :, pl.ds(64 * h, 64), :], dst(c), field_recv.at[n, c]
                ).start()

            @pl.when(jnp.logical_not(stays(h)))
            def _():
                field_copy(n, h).start()

    def field_wait(n):
        src, dst = field_parts(n)
        for core in range(2):
            landed(dst(core), field_recv.at[n, core])

    for n in range(5):
        pad[n, 0:4] = jnp.zeros((4, 80, 128), F32)
        pad[n, 12:16] = jnp.zeros((4, 80, 128), F32)
        pad[n, 4:12, 0:8] = jnp.zeros((8, 8, 128), F32)
        pad[n, 4:12, 72:80] = jnp.zeros((8, 8, 128), F32)
        sides[n, :, 8:16] = jnp.zeros((8, 8, 128), F32)

    @pl.when(yh == 0)
    def _():
        for n in range(5):
            sides[n, :, 4:8] = jnp.zeros((8, 4, 128), F32)

    @pl.when(yh == 1)
    def _():
        for n in range(5):
            sides[n, :, 16:20] = jnp.zeros((8, 4, 128), F32)

    for side, first_or_last in ((0, 0), (1, 15)):

        @pl.when(k == first_or_last)
        def _():
            for n in range(5):
                ends[n, side] = jnp.zeros((4, 64, 128), F32)

    square = lax.broadcasted_iota(I32, (64, 64), 0) == lax.broadcasted_iota(I32, (64, 64), 1)

    def upright(row):
        return jnp.sum(
            jnp.where(square, jnp.broadcast_to(row.astype(F32), (64, 64)), 0.0),
            axis=1, keepdims=True,
        )

    row_of = receivers[0] - 8 * k
    col_of = receivers[1] - 64 * yh
    inside = (row_of >= 0) & (row_of < 8) & (col_of >= 0) & (col_of < 64)
    flat = upright(jnp.where(inside, row_of * 64 + col_of, -1))
    hits[...] = jnp.where(
        lax.broadcasted_iota(I32, (64, 512), 1).astype(F32) == flat, 1.0, 0.0
    ).astype(F32)
    deeps[...] = jnp.where(
        lax.broadcasted_iota(I32, (64, 128), 1).astype(F32) == upright(receivers[2]), 1.0, 0.0
    ).astype(F32)
    for n in range(3):
        seens[n] = upright(observed[n])
    apart = jnp.abs(
        lax.broadcasted_iota(I32, (128, 128), 0) - lax.broadcasted_iota(I32, (128, 128), 1)
    )
    line = jnp.where(apart == 0, 3.0 * COEF[0], 0.0)
    for reach in range(1, 5):
        line = jnp.where(apart == reach, COEF[reach], line)
    band[...] = line.astype(F32)
    s_row, s_col, s_dep = source[0, 0] - 8 * k, source[0, 1] - 64 * yh, source[0, 2]
    spot[...] = jnp.where(
        (lax.broadcasted_iota(I32, (8, 64, 128), 0) == s_row)
        & (lax.broadcasted_iota(I32, (8, 64, 128), 1) == s_col)
        & (lax.broadcasted_iota(I32, (8, 64, 128), 2) == s_dep),
        1.0, 0.0,
    ).astype(F32)

    def record(field, n):
        lines = jnp.dot(
            hits[...], field.reshape(512, 128), precision=HIGH, preferred_element_type=F32
        )
        return jnp.sum(lines * deeps[...], axis=1, keepdims=True) - seens[n]

    def inject(residual):
        return lax.dot_general(
            hits[...], deeps[...] * residual, (((0,), (0,)), ((), ())),
            precision=HIGH, preferred_element_type=F32,
        ).reshape(8, 64, 128)

    def end_copy(n, way):
        return push(
            pad.at[n, pl.ds(4 + 4 * way, 4), pl.ds(8, 64)], ends.at[n, 1 - way],
            halo_send.at[n, way], halo_recv.at[n, way], at_k((k + 15 + 2 * way) % 16),
        )

    def side_copy(n, half_of):
        return push(
            pad.at[n, pl.ds(4, 8), pl.ds(68 - 60 * half_of, 4)],
            sides.at[n, :, pl.ds(4 + 12 * half_of, 4)],
            halo_send.at[n, 2], halo_recv.at[n, 2], partner,
        )

    def end_there(way):
        return k > 0 if way == 0 else k < 15

    def end_start(n, way):
        @pl.when(end_there(way))
        def _():
            end_copy(n, way).start()

    def side_start(n):
        for half_of in range(2):

            @pl.when(yh == half_of)
            def _():
                side_copy(n, half_of).start()

    def halo_start(n):
        side_start(n)
        for way in range(2):
            end_start(n, way)

    def halo_wait(n):
        for way in range(2):

            @pl.when(end_there(1 - way))
            def _():
                landed(ends.at[n, 1 - way], halo_recv.at[n, way])

        for half_of in range(2):

            @pl.when(yh != half_of)
            def _():
                landed(sides.at[n, :, pl.ds(4 + 12 * half_of, 4)], halo_recv.at[n, 2])

    def halo_done(n):
        for way in range(2):

            @pl.when(end_there(way))
            def _():
                end_copy(n, way).wait_send()

        for half_of in range(2):

            @pl.when(yh == half_of)
            def _():
                side_copy(n, half_of).wait_send()

    def close(n, lap, new, weight, send):
        def add(row, at, wide, extra):
            if lap is not None:
                lap[row, pl.ds(at, wide)] = lap[row, pl.ds(at, wide)] + extra
            below, right = (4, 8) if send else (0, 0)
            place = pl.ds(pl.multiple_of(right + at, 8), wide)
            new[below + row, place] = new[below + row, place] + weight[row, pl.ds(at, wide)] * extra

        def from_end(way, i, at, wide):
            total = None
            for d in range(i + 1, 5):
                row = 4 + i - d if way == 0 else d - i - 1
                term = COEF[d] * ends[n, way, row, pl.ds(at, wide)]
                total = term if total is None else total + term
            return total

        beside = None
        for d in range(1, 5):
            term = COEF[d] * (sides[n, :, 8 - d : 16 - d] + sides[n, :, 8 + d : 16 + d])
            beside = term if beside is None else beside + term
        edge = pl.multiple_of(56 - 56 * yh, 8)
        rest = pl.multiple_of(8 * yh, 8)
        for way in range(2):
            for i in range(4):
                row = i if way == 0 else 7 - i
                add(row, edge, 8, beside[row] + from_end(way, i, edge, 8))
        if send:
            side_start(n + 1)

        def rows_of(way):
            for i in range(4):
                row = i if way == 0 else 7 - i
                add(row, rest, 56, from_end(way, i, rest, 56))
            if send:
                end_start(n + 1, way)

        @pl.when(c == 0)
        def _():
            rows_of(0)
            rows_of(1)

        @pl.when(c == 1)
        def _():
            rows_of(1)
            rows_of(0)

    def laplace(n):
        total = jnp.dot(
            pad[n, 4:12, 8:72].reshape(512, 128), band[...],
            precision=HIGH, preferred_element_type=F32,
        ).reshape(8, 64, 128)
        for d in range(1, 5):
            beside = pad[n, 4 - d : 12 - d, 8:72] + pad[n, 4 + d : 12 + d, 8:72]
            beside += pad[n, 4:12, 8 - d : 72 - d] + pad[n, 4:12, 8 + d : 72 + d]
            total += COEF[d] * beside
        return total

    own_model.wait()
    for d in (1, 2, 3):
        landed(anchors.at[(x + 4 - d) % 4], a_recv.at[d])

    def super_of(other, g):
        start = anchors[other, part(g), :]
        residue = 32 * x + lax.broadcasted_iota(I32, (32, WIDE, 128), 0)
        return (start >> 7)[None] + jnp.where(residue < (start & 127)[None], 1, 0)

    def x_copy(g, d):
        return push(
            picked.at[d, :, part(g), :],
            rows[g].at[pl.ds(pl.multiple_of(32 * x, 32), 32), part(g), :],
            x_send.at[g, d], x_recv.at[g, d], at_x((x + d) % 4),
        )

    for g in range(PARTS):
        landed(gath.at[(yl + 2) % 4, :, part(g), :], y_recv.at[g, 2])

        @pl.when(inner)
        def _():
            y_relay(g).start()

        for d in (1, 3):
            landed(gath.at[(yl + 4 - d) % 4, :, part(g), :], y_recv.at[g, d])
        for d in (2, 1, 3, 0):
            which = super_of((x + d) % 4, g)
            chosen = gath[0, :, part(g), :]
            for q in range(1, 4):
                chosen = jnp.where(which == q, gath[q, :, part(g), :], chosen)
            if d:
                picked[d, :, part(g), :] = chosen
                x_copy(g, d).start()
            else:
                rows[g][pl.ds(pl.multiple_of(32 * x, 32), 32), part(g), :] = chosen
    field_start(0)
    field_start(1)

    first = ox & 127

    def s_copy(g, d):
        return push(
            rowsend.at[d, :, part(g), :], cols[g].at[k, :, part(g), :],
            s_send.at[g, d], s_recv.at[g, d], at_k((k + d) % 16),
        )

    for g in range(PARTS):
        for d in (1, 3, 2):
            landed(
                rows[g].at[pl.ds(pl.multiple_of(32 * ((x + 4 - d) % 4), 32), 32), part(g), :],
                x_recv.at[g, d],
            )

        def spread(n, carry):
            d = (n + 8) % 16
            other = (k + d) % 16
            for r in range(8):
                rowsend[d, r, part(g), :] = rows[g][(first + 8 * other + r) & 127, part(g), :]
            s_copy(g, d).start()
            return carry

        lax.fori_loop(0, 8, spread, 0)
        lax.fori_loop(9, 16, spread, 0)
        for r in range(8):
            cols[g][k, r, part(g), :] = rows[g][(first + 8 * k + r) & 127, part(g), :]

    turn = oy & 63

    def columns(h, e, core, g):
        at = (oy >> 6) + h
        place = 32 * e + 16 * yh + 8 * core + WIDE * g + lax.broadcasted_iota(I32, (8, WIDE, 128), 1)
        low = cols[g][4 * at + 2 * e + core, :, part(g), :]
        high = cols[g][4 * jnp.minimum(at + 1, 3) + 2 * e + core, :, part(g), :]
        return jnp.where(place < turn, high, low)

    def h_copy(g):
        return push(
            halfsend.at[:, :, :, part(g), :], half.at[yh, :, :, :, part(g), :],
            h_send.at[g], h_recv.at[g], partner,
        )

    for g in range(PARTS):

        def spread_in(d, carry):
            landed(cols[g].at[(k + 16 - d) % 16, :, part(g), :], s_recv.at[g, d])
            return carry

        lax.fori_loop(1, 16, spread_in, 0)
        for e in range(2):
            for core in range(2):
                halfsend[e, core, :, part(g), :] = columns(1 - yh, e, core, g)
        h_copy(g).start()
        for e in range(2):
            for core in range(2):
                half[yh, e, core, :, part(g), :] = columns(yh, e, core, g)
        if g == 0:
            field_wait(0)
            halo_start(0)
    field_start(2)
    field_start(3)
    laps[0] = laplace(0)
    field_wait(1)
    pad[1, 4:12, 8:72] = 2.0 * pad[0, 4:12, 8:72] - before[...] + wavelet[0, 0] * spot[...]
    third[...] = jnp.zeros((8, 64, 128), F32)
    halo_wait(0)
    close(0, laps.at[0], third, spot, False)
    for g in range(PARTS):
        landed(half.at[1 - yh, :, :, :, part(g), :], h_recv.at[g])
    for e in range(2):
        for b in range(2):
            for core in range(2):
                t = 4 * e + 2 * b + core
                twice[:, 8 * t : 8 * t + 8] = half[b, e, core]
                twice[:, 64 + 8 * t : 72 + 8 * t] = half[b, e, core]
    for r in range(8):
        speed[r] = twice[r, pl.ds(turn, 64)]

    pad[1, 4:12, 8:72] = pad[1, 4:12, 8:72] + speed[...] * laps[0]
    halo_start(1)
    laps[1] = laplace(1)
    pad[2, 4:12, 8:72] = (
        2.0 * pad[1, 4:12, 8:72] - pad[0, 4:12, 8:72] + wavelet[0, 1] * spot[...]
        + speed[...] * laps[1]
    )
    residual0 = record(pad[1, 4:12, 8:72], 0)
    halo_wait(1)
    close(1, laps.at[1], pad.at[2], speed, True)
    laps[2] = laplace(2)
    third[...] = (
        2.0 * pad[2, 4:12, 8:72] - pad[1, 4:12, 8:72] + wavelet[0, 2] * spot[...]
        + speed[...] * laps[2]
    )
    residual1 = record(pad[2, 4:12, 8:72], 1)
    halo_wait(2)
    close(2, laps.at[2], third, speed, False)
    residual2 = record(third[...], 2)

    field_wait(2)
    adj[0] = after_now[...] + inject(residual2)
    pad[3, 4:12, 8:72] = speed[...] * adj[0]
    halo_start(3)
    field_wait(3)
    adj[1] = 2.0 * adj[0] - after[...] + inject(residual1) + laplace(3)
    pad[4, 4:12, 8:72] = speed[...] * adj[1]
    images[:, 0:64] = adj[0] * laps[2]
    halo_wait(3)
    close(3, adj.at[1], pad.at[4], speed, True)
    third[...] = 2.0 * adj[1] - adj[0] + inject(residual0) + laplace(4)
    images[:, 0:64] = images[:, 0:64] + adj[1] * laps[1] + third[...] * laps[0]
    halo_wait(4)
    close(4, None, images, laps.at[0], False)
    images[:, 64:128] = images[:, 0:64]

    for r in range(8):
        line = images[r, pl.ds(64 - turn, 64)]
        for e in range(2):
            for b in range(2):
                for core in range(2):
                    t = 4 * e + 2 * b + core
                    back_half[b, e, core, r] = line[8 * t : 8 * t + 8]

    def bh_copy(g):
        return push(
            back_half.at[1 - yh, :, :, :, part(g), :], back_in.at[:, :, :, part(g), :],
            bh_send.at[g], bh_recv.at[g], partner,
        )

    for g in range(PARTS):
        bh_copy(g).start()

    def owned(other, g):
        zz, core = other // 2, other % 2
        e, q = zz % 2, zz // 2
        place = 32 * e + 16 * yh + 8 * core + WIDE * g + lax.broadcasted_iota(I32, (WIDE, 128), 0)
        wraps = jnp.where(place < turn, 1, 0)
        mine = (wraps + ((oy >> 6) + yh) == q)[None]
        theirs = (wraps + ((oy >> 6) + 1 - yh) == q)[None]
        return jnp.where(mine, back_half[yh, e, core, :, part(g), :], 0.0) + jnp.where(
            theirs, back_in[e, core, :, part(g), :], 0.0
        )

    def bs_copy(g, d):
        return push(
            back_send.at[d, :, part(g), :],
            back_rows[g].at[pl.ds(pl.multiple_of(8 * k, 8), 8), part(g), :],
            bs_send.at[g, d], bs_recv.at[g, d], at_k((k + d) % 16),
        )

    for g in range(PARTS):
        landed(back_in.at[:, :, :, part(g), :], bh_recv.at[g])

        def give(n, carry):
            d = (n + 8) % 16
            back_send[d, :, part(g), :] = owned((k + d) % 16, g)
            bs_copy(g, d).start()
            return carry

        lax.fori_loop(0, 8, give, 0)
        lax.fori_loop(9, 16, give, 0)
        back_rows[g][pl.ds(pl.multiple_of(8 * k, 8), 8), part(g), :] = owned(k, g)

    def bx_copy(g, d):
        return push(
            back_pick.at[d, :, part(g), :], back_in_x.at[x, :, part(g), :],
            bx_send.at[g, d], bx_recv.at[g, d], at_x((x + d) % 4),
        )

    for g in range(PARTS):

        def given(d, carry):
            landed(
                back_rows[g].at[
                    pl.ds(pl.multiple_of(8 * ((k + 16 - d) % 16), 8), 8), part(g), :
                ],
                bs_recv.at[g, d],
            )
            return carry

        lax.fori_loop(1, 16, given, 0)
        for d in (2, 1, 3, 0):
            other = (x + d) % 4

            def turned(n, carry):
                for r in range(8):
                    i = 8 * n + r
                    back_pick[d, i, part(g), :] = back_rows[g][
                        (32 * other + i + 128 - first) & 127, part(g), :
                    ]
                return carry

            lax.fori_loop(0, 4, turned, 0)
            if d:
                bx_copy(g, d).start()
            else:
                back_in_x[x, :, part(g), :] = back_pick[0, :, part(g), :]

    def by_copy(g, d):
        return push(
            back_sum.at[d, :, part(g), :], back_in_y.at[d, :, part(g), :],
            by_send.at[g, d], by_recv.at[g, d], at_y((yl + d) % 4),
        )

    for g in range(PARTS):
        for d in (1, 3, 2):
            landed(back_in_x.at[(x + 4 - d) % 4, :, part(g), :], bx_recv.at[g, d])
        for d in (2, 1, 3, 0):
            total = jnp.zeros((32, WIDE, 128), F32)
            for other in range(4):
                total += jnp.where(
                    super_of(other, g) == (yl + d) % 4, back_in_x[other, :, part(g), :], 0.0
                )
            back_sum[d, :, part(g), :] = total
            if d:
                by_copy(g, d).start()
    for g in range(PARTS):
        for d in (1, 2, 3):
            landed(back_in_y.at[d, :, part(g), :], by_recv.at[g, d])
    out[...] = back_sum[0] + back_in_y[1] + back_in_y[2] + back_in_y[3]

    for d in (1, 2, 3):
        a_copy(d).wait_send()
    for g in range(PARTS):
        for d in (1, 2, 3):

            @pl.when(y_direct(d))
            def _():
                y_copy(g, d).wait_send()

            x_copy(g, d).wait_send()
            bx_copy(g, d).wait_send()
            by_copy(g, d).wait_send()

        def left(d, carry):
            s_copy(g, d).wait_send()
            bs_copy(g, d).wait_send()
            return carry

        lax.fori_loop(1, 16, left, 0)
        h_copy(g).wait_send()
        bh_copy(g).wait_send()

        @pl.when(inner)
        def _():
            y_relay(g).wait_send()
    for n in range(5):
        halo_done(n)
    for n in range(4):
        for h in range(2):

            @pl.when(jnp.logical_not(stays(h)))
            def _():
                field_copy(n, h).wait_send()


def on_device(
    courant, anchor, source, wavelet, receivers, observed,
    wave_before, wave_now, adjoint_after, adjoint_now,
):
    vmem, smem = pltpu.VMEM, pltpu.SMEM
    dma = pltpu.SemaphoreType.DMA
    return pl.pallas_call(
        kernel,
        out_shape=jax.ShapeDtypeStruct((32, 8, 128), F32),
        in_specs=[pl.BlockSpec(memory_space=pltpu.HBM)] * 10,
        out_specs=pl.BlockSpec(memory_space=vmem),
        scratch_shapes=[
            vmem((4, 32, 8, 128), F32),
            vmem((4, 32, 8, 128), F32),
            vmem((128, 8, 128), F32),
            vmem((128, 8, 128), F32),
            vmem((16, 8, 8, 128), F32),
            vmem((16, 8, 8, 128), F32),
            vmem((16, 8, 8, 128), F32),
            vmem((2, 2, 8, 8, 128), F32),
            vmem((2, 2, 2, 8, 8, 128), F32),
            vmem((8, 128, 128), F32),
            vmem((8, 64, 128), F32),
            vmem((5, 16, 80, 128), F32),
            vmem((5, 2, 4, 64, 128), F32),
            vmem((5, 8, 24, 128), F32),
            vmem((8, 64, 128), F32),
            vmem((8, 64, 128), F32),
            vmem((8, 64, 128), F32),
            vmem((3, 8, 64, 128), F32),
            vmem((8, 64, 128), F32),
            vmem((2, 8, 64, 128), F32),
            vmem((8, 64, 128), F32),
            vmem((8, 128, 128), F32),
            vmem((2, 2, 2, 8, 8, 128), F32),
            vmem((2, 2, 8, 8, 128), F32),
            vmem((16, 8, 8, 128), F32),
            vmem((128, 8, 128), F32),
            vmem((128, 8, 128), F32),
            vmem((4, 32, 8, 128), F32),
            vmem((4, 32, 8, 128), F32),
            vmem((4, 32, 8, 128), F32),
            vmem((4, 32, 8, 128), F32),
            vmem((4, 8, 128), I32),
            vmem((8, 128), I32),
            smem((1, 2), I32),
            smem((1, 3), I32),
            smem((1, 3), F32),
            vmem((3, 1, 64), I32),
            vmem((3, 1, 64), F32),
            vmem((128, 128), F32),
            vmem((64, 512), F32),
            vmem((64, 128), F32),
            vmem((3, 64, 1), F32),
            dma((6,)),
            dma((4, 2)), dma((4, 2)),
            dma((PARTS, 4)), dma((PARTS, 4)),
            dma((4,)), dma((4,)),
            dma((PARTS, 4)), dma((PARTS, 4)),
            dma((PARTS, 16)), dma((PARTS, 16)),
            dma((PARTS,)), dma((PARTS,)),
            dma((5, 3)), dma((5, 3)),
            dma((PARTS,)), dma((PARTS,)),
            dma((PARTS, 16)), dma((PARTS, 16)),
            dma((PARTS, 4)), dma((PARTS, 4)),
            dma((PARTS, 4)), dma((PARTS, 4)),
            dma((PARTS,)),
        ],
        compiler_params=pltpu.CompilerParams(
            collective_id=0, has_side_effects=True, vmem_limit_bytes=60 * 1024 * 1024
        ),
    )(
        anchor, source, wavelet, receivers.transpose(2, 0, 1), observed.transpose(1, 0, 2), courant,
        wave_before, wave_now, adjoint_after, adjoint_now,
    )


def solution(mesh):
    return jax.shard_map(
        on_device,
        mesh=mesh,
        in_specs=(
            P("shot", "space", None),
            P("shot", None),
            P("shot", None),
            P("shot", None),
            P("shot", None, None),
            P("shot", None, None),
            P("shot", "space", None, None),
            P("shot", "space", None, None),
            P("shot", "space", None, None),
            P("shot", "space", None, None),
        ),
        out_specs=P("shot", "space", None),
        check_vma=False,
    )
```

```python
import jax
import jax.numpy as jnp
from jax import lax
from jax.experimental import pallas as pl
from jax.experimental.pallas import tpu as pltpu
from jax.sharding import PartitionSpec as P

MESH = pl.DeviceIdType.MESH
HIGH = lax.Precision.HIGHEST
COEF = (-205.0 / 72.0, 8.0 / 5.0, -1.0 / 5.0, 8.0 / 315.0, -1.0 / 560.0)
F32 = jnp.float32
I32 = jnp.int32
PARTS = 2
WIDE = 8 // PARTS


def kernel(
    anchor_in, source_in, wavelet_in, receivers_in, observed_in, courant, wave_before, wave_now,
    adjoint_after, adjoint_now, out,
    gath, picked, rows_0, rows_1, rowsend, cols_0, cols_1, halfsend, half, twice, speed,
    pad, ends, sides, before, after_now, after, laps, third, adj, spot, images,
    back_half, back_in, back_send, back_rows_0, back_rows_1, back_pick, back_in_x, back_sum, back_in_y,
    anchors, anchor_own, anchor, source, wavelet, receivers, observed, band, hits, deeps, seens,
    local_sem, field_send, field_recv, y_send, y_recv, a_send, a_recv, x_send, x_recv,
    s_send, s_recv, h_send, h_recv, halo_send, halo_recv,
    bh_send, bh_recv, bs_send, bs_recv, bx_send, bx_recv, by_send, by_recv, relay_send,
):
    rows, cols, back_rows = (rows_0, rows_1), (cols_0, cols_1), (back_rows_0, back_rows_1)
    shot = lax.axis_index("shot")
    space = lax.axis_index("space")
    yl, x = shot // 4, shot % 4
    z, yh, c = space // 4, (space // 2) % 2, space % 2
    k = 2 * z + c

    def at_k(other):
        return (shot, (other // 2) * 4 + yh * 2 + other % 2)

    def at_x(other):
        return (yl * 4 + other, space)

    def at_y(other):
        return (other * 4 + x, space)

    partner = (shot, z * 4 + (1 - yh) * 2 + c)
    diagonal = (shot, z * 4 + (1 - yh) * 2 + (1 - c))

    def push(src, dst, send, recv, device):
        return pltpu.make_async_remote_copy(
            src_ref=src, dst_ref=dst, send_sem=send, recv_sem=recv,
            device_id=device, device_id_type=MESH,
        )

    def landed(dst, sem):
        pltpu.make_async_copy(dst, dst, sem).wait()

    barrier = pltpu.get_barrier_semaphore()
    for d in range(1, 4):
        pl.semaphore_signal(barrier, 1, device_id=at_x((x + d) % 4), device_id_type=MESH)
        pl.semaphore_signal(barrier, 1, device_id=at_y((yl + d) % 4), device_id_type=MESH)
    for d in range(1, 16):
        pl.semaphore_signal(barrier, 1, device_id=at_k((k + d) % 16), device_id_type=MESH)
    pl.semaphore_signal(barrier, 1, device_id=partner, device_id_type=MESH)
    pl.semaphore_signal(barrier, 1, device_id=diagonal, device_id_type=MESH)
    small = [
        pltpu.make_async_copy(src, dst, local_sem.at[1 + n])
        for n, (src, dst) in enumerate(
            (
                (anchor_in, anchor), (source_in, source), (wavelet_in, wavelet),
                (receivers_in, receivers), (observed_in, observed),
            )
        )
    ]
    for copy in small:
        copy.start()

    for copy in small:
        copy.wait()
    ox, oy = anchor[0, 0], anchor[0, 1]
    anchor_own[...] = jnp.full((8, 128), ox, I32)
    anchors[x] = jnp.full((8, 128), ox, I32)


    pl.semaphore_wait(barrier, 23)

    def part(g):
        return pl.ds(WIDE * g, WIDE)

    def y_copy(g, d):
        return push(
            courant.at[:, part(g), :], gath.at[yl, :, part(g), :],
            y_send.at[g, d], y_recv.at[g, d], at_y((yl + d) % 4),
        )

    own_model = pltpu.make_async_copy(courant, gath.at[yl], local_sem.at[0])
    own_model.start()

    def y_direct(d):
        if d == 2:
            return yl >= 0
        return yl != (0 if d == 3 else 3)

    inner = jnp.logical_and(yl > 0, yl < 3)

    def y_relay(g):
        slot = gath.at[(yl + 2) % 4, :, part(g), :]
        return push(slot, slot, relay_send.at[g], y_recv.at[g, 2 * yl - 1], at_y(3 * (yl - 1)))

    def a_copy(d):
        return push(anchor_own, anchors.at[x], a_send.at[d], a_recv.at[d], at_x((x + d) % 4))

    for d in (1, 2, 3):
        a_copy(d).start()
    for g in range(PARTS):
        for d in (2, 1, 3):

            @pl.when(y_direct(d))
            def _():
                y_copy(g, d).start()

    def field_parts(n):
        src = (wave_now, wave_before, adjoint_now, adjoint_after)[n]

        def dst(core):
            if n == 0:
                return pad.at[0, pl.ds(4 + 4 * core, 4), pl.ds(8, 64)]
            return (before, after_now, after)[n - 1].at[pl.ds(4 * core, 4)]

        return src, dst

    def field_copy(n, h):
        src, dst = field_parts(n)
        return push(
            src.at[0, :, pl.ds(64 * h, 64), :], dst(c), field_send.at[n, h], field_recv.at[n, c],
            (shot, z * 4 + 2 * h + yh),
        )

    def stays(h):
        return jnp.logical_and(yh == h, c == h)

    def field_start(n):
        src, dst = field_parts(n)
        for h in range(2):

            @pl.when(stays(h))
            def _():
                pltpu.make_async_copy(
                    src.at[0, :, pl.ds(64 * h, 64), :], dst(c), field_recv.at[n, c]
                ).start()

            @pl.when(jnp.logical_not(stays(h)))
            def _():
                field_copy(n, h).start()

    def field_wait(n):
        src, dst = field_parts(n)
        for core in range(2):
            landed(dst(core), field_recv.at[n, core])

    for n in range(5):
        pad[n, 0:4] = jnp.zeros((4, 80, 128), F32)
        pad[n, 12:16] = jnp.zeros((4, 80, 128), F32)
        pad[n, 4:12, 0:8] = jnp.zeros((8, 8, 128), F32)
        pad[n, 4:12, 72:80] = jnp.zeros((8, 8, 128), F32)
        sides[n, :, 8:16] = jnp.zeros((8, 8, 128), F32)

    @pl.when(yh == 0)
    def _():
        for n in range(5):
            sides[n, :, 4:8] = jnp.zeros((8, 4, 128), F32)

    @pl.when(yh == 1)
    def _():
        for n in range(5):
            sides[n, :, 16:20] = jnp.zeros((8, 4, 128), F32)

    for side, first_or_last in ((0, 0), (1, 15)):

        @pl.when(k == first_or_last)
        def _():
            for n in range(5):
                ends[n, side] = jnp.zeros((4, 64, 128), F32)

    square = lax.broadcasted_iota(I32, (64, 64), 0) == lax.broadcasted_iota(I32, (64, 64), 1)

    def upright(row):
        return jnp.sum(
            jnp.where(square, jnp.broadcast_to(row.astype(F32), (64, 64)), 0.0),
            axis=1, keepdims=True,
        )

    row_of = receivers[0] - 8 * k
    col_of = receivers[1] - 64 * yh
    inside = (row_of >= 0) & (row_of < 8) & (col_of >= 0) & (col_of < 64)
    flat = upright(jnp.where(inside, row_of * 64 + col_of, -1))
    hits[...] = jnp.where(
        lax.broadcasted_iota(I32, (64, 512), 1).astype(F32) == flat, 1.0, 0.0
    ).astype(F32)
    deeps[...] = jnp.where(
        lax.broadcasted_iota(I32, (64, 128), 1).astype(F32) == upright(receivers[2]), 1.0, 0.0
    ).astype(F32)
    for n in range(3):
        seens[n] = upright(observed[n])
    apart = jnp.abs(
        lax.broadcasted_iota(I32, (128, 128), 0) - lax.broadcasted_iota(I32, (128, 128), 1)
    )
    line = jnp.where(apart == 0, 3.0 * COEF[0], 0.0)
    for reach in range(1, 5):
        line = jnp.where(apart == reach, COEF[reach], line)
    band[...] = line.astype(F32)
    s_row, s_col, s_dep = source[0, 0] - 8 * k, source[0, 1] - 64 * yh, source[0, 2]
    spot[...] = jnp.where(
        (lax.broadcasted_iota(I32, (8, 64, 128), 0) == s_row)
        & (lax.broadcasted_iota(I32, (8, 64, 128), 1) == s_col)
        & (lax.broadcasted_iota(I32, (8, 64, 128), 2) == s_dep),
        1.0, 0.0,
    ).astype(F32)

    def record(field, n):
        lines = jnp.dot(
            hits[...], field.reshape(512, 128), precision=HIGH, preferred_element_type=F32
        )
        return jnp.sum(lines * deeps[...], axis=1, keepdims=True) - seens[n]

    def inject(residual):
        return lax.dot_general(
            hits[...], deeps[...] * residual, (((0,), (0,)), ((), ())),
            precision=HIGH, preferred_element_type=F32,
        ).reshape(8, 64, 128)

    def end_copy(n, way):
        return push(
            pad.at[n, pl.ds(4 + 4 * way, 4), pl.ds(8, 64)], ends.at[n, 1 - way],
            halo_send.at[n, way], halo_recv.at[n, way], at_k((k + 15 + 2 * way) % 16),
        )

    def side_copy(n, half_of):
        return push(
            pad.at[n, pl.ds(4, 8), pl.ds(68 - 60 * half_of, 4)],
            sides.at[n, :, pl.ds(4 + 12 * half_of, 4)],
            halo_send.at[n, 2], halo_recv.at[n, 2], partner,
        )

    def end_there(way):
        return k > 0 if way == 0 else k < 15

    def end_start(n, way):
        @pl.when(end_there(way))
        def _():
            end_copy(n, way).start()

    def side_start(n):
        for half_of in range(2):

            @pl.when(yh == half_of)
            def _():
                side_copy(n, half_of).start()

    def halo_start(n):
        side_start(n)
        for way in range(2):
            end_start(n, way)

    def halo_wait(n):
        for way in range(2):

            @pl.when(end_there(1 - way))
            def _():
                landed(ends.at[n, 1 - way], halo_recv.at[n, way])

        for half_of in range(2):

            @pl.when(yh != half_of)
            def _():
                landed(sides.at[n, :, pl.ds(4 + 12 * half_of, 4)], halo_recv.at[n, 2])

    def halo_done(n):
        for way in range(2):

            @pl.when(end_there(way))
            def _():
                end_copy(n, way).wait_send()

        for half_of in range(2):

            @pl.when(yh == half_of)
            def _():
                side_copy(n, half_of).wait_send()

    def close(n, lap, new, weight, send):
        def add(row, at, wide, extra):
            if lap is not None:
                lap[row, pl.ds(at, wide)] = lap[row, pl.ds(at, wide)] + extra
            below, right = (4, 8) if send else (0, 0)
            place = pl.ds(pl.multiple_of(right + at, 8), wide)
            new[below + row, place] = new[below + row, place] + weight[row, pl.ds(at, wide)] * extra

        def from_end(way, i, at, wide):
            total = None
            for d in range(i + 1, 5):
                row = 4 + i - d if way == 0 else d - i - 1
                term = COEF[d] * ends[n, way, row, pl.ds(at, wide)]
                total = term if total is None else total + term
            return total

        beside = None
        for d in range(1, 5):
            term = COEF[d] * (sides[n, :, 8 - d : 16 - d] + sides[n, :, 8 + d : 16 + d])
            beside = term if beside is None else beside + term
        edge = pl.multiple_of(56 - 56 * yh, 8)
        rest = pl.multiple_of(8 * yh, 8)
        for way in range(2):
            for i in range(4):
                row = i if way == 0 else 7 - i
                add(row, edge, 8, beside[row] + from_end(way, i, edge, 8))
        if send:
            side_start(n + 1)

        def rows_of(way):
            for i in range(4):
                row = i if way == 0 else 7 - i
                add(row, rest, 56, from_end(way, i, rest, 56))
            if send:
                end_start(n + 1, way)

        @pl.when(c == 0)
        def _():
            rows_of(0)
            rows_of(1)

        @pl.when(c == 1)
        def _():
            rows_of(1)
            rows_of(0)

    def laplace(n):
        total = jnp.dot(
            pad[n, 4:12, 8:72].reshape(512, 128), band[...],
            precision=HIGH, preferred_element_type=F32,
        ).reshape(8, 64, 128)
        for d in range(1, 5):
            beside = pad[n, 4 - d : 12 - d, 8:72] + pad[n, 4 + d : 12 + d, 8:72]
            beside += pad[n, 4:12, 8 - d : 72 - d] + pad[n, 4:12, 8 + d : 72 + d]
            total += COEF[d] * beside
        return total

    own_model.wait()
    for d in (1, 2, 3):
        landed(anchors.at[(x + 4 - d) % 4], a_recv.at[d])

    def super_of(other, g):
        start = anchors[other, part(g), :]
        residue = 32 * x + lax.broadcasted_iota(I32, (32, WIDE, 128), 0)
        return (start >> 7)[None] + jnp.where(residue < (start & 127)[None], 1, 0)

    def x_copy(g, d):
        return push(
            picked.at[d, :, part(g), :],
            rows[g].at[pl.ds(pl.multiple_of(32 * x, 32), 32), part(g), :],
            x_send.at[g, d], x_recv.at[g, d], at_x((x + d) % 4),
        )

    for g in range(PARTS):
        landed(gath.at[(yl + 2) % 4, :, part(g), :], y_recv.at[g, 2])

        @pl.when(inner)
        def _():
            y_relay(g).start()

        for d in (1, 3):
            landed(gath.at[(yl + 4 - d) % 4, :, part(g), :], y_recv.at[g, d])
        for d in (2, 1, 3, 0):
            which = super_of((x + d) % 4, g)
            chosen = gath[0, :, part(g), :]
            for q in range(1, 4):
                chosen = jnp.where(which == q, gath[q, :, part(g), :], chosen)
            if d:
                picked[d, :, part(g), :] = chosen
                x_copy(g, d).start()
            else:
                rows[g][pl.ds(pl.multiple_of(32 * x, 32), 32), part(g), :] = chosen
    field_start(0)
    field_start(1)

    first = ox & 127

    def s_copy(g, d):
        return push(
            rowsend.at[d, :, part(g), :], cols[g].at[k, :, part(g), :],
            s_send.at[g, d], s_recv.at[g, d], at_k((k + d) % 16),
        )

    for g in range(PARTS):
        for d in (1, 3, 2):
            landed(
                rows[g].at[pl.ds(pl.multiple_of(32 * ((x + 4 - d) % 4), 32), 32), part(g), :],
                x_recv.at[g, d],
            )

        def spread(n, carry):
            d = (n + 8) % 16
            other = (k + d) % 16
            for r in range(8):
                rowsend[d, r, part(g), :] = rows[g][(first + 8 * other + r) & 127, part(g), :]
            s_copy(g, d).start()
            return carry

        lax.fori_loop(0, 8, spread, 0)
        lax.fori_loop(9, 16, spread, 0)
        for r in range(8):
            cols[g][k, r, part(g), :] = rows[g][(first + 8 * k + r) & 127, part(g), :]

    turn = oy & 63

    def columns(h, e, core, g):
        at = (oy >> 6) + h
        place = 32 * e + 16 * yh + 8 * core + WIDE * g + lax.broadcasted_iota(I32, (8, WIDE, 128), 1)
        low = cols[g][4 * at + 2 * e + core, :, part(g), :]
        high = cols[g][4 * jnp.minimum(at + 1, 3) + 2 * e + core, :, part(g), :]
        return jnp.where(place < turn, high, low)

    def h_copy(g):
        return push(
            halfsend.at[:, :, :, part(g), :], half.at[yh, :, :, :, part(g), :],
            h_send.at[g], h_recv.at[g], partner,
        )

    for g in range(PARTS):

        def spread_in(d, carry):
            landed(cols[g].at[(k + 16 - d) % 16, :, part(g), :], s_recv.at[g, d])
            return carry

        lax.fori_loop(1, 16, spread_in, 0)
        for e in range(2):
            for core in range(2):
                halfsend[e, core, :, part(g), :] = columns(1 - yh, e, core, g)
        h_copy(g).start()
        for e in range(2):
            for core in range(2):
                half[yh, e, core, :, part(g), :] = columns(yh, e, core, g)
    field_wait(0)
    halo_start(0)
    field_start(2)
    field_start(3)
    laps[0] = laplace(0)
    field_wait(1)
    pad[1, 4:12, 8:72] = 2.0 * pad[0, 4:12, 8:72] - before[...] + wavelet[0, 0] * spot[...]
    third[...] = jnp.zeros((8, 64, 128), F32)
    halo_wait(0)
    close(0, laps.at[0], third, spot, False)
    for g in range(PARTS):
        landed(half.at[1 - yh, :, :, :, part(g), :], h_recv.at[g])
    for e in range(2):
        for b in range(2):
            for core in range(2):
                t = 4 * e + 2 * b + core
                twice[:, 8 * t : 8 * t + 8] = half[b, e, core]
                twice[:, 64 + 8 * t : 72 + 8 * t] = half[b, e, core]
    for r in range(8):
        speed[r] = twice[r, pl.ds(turn, 64)]

    pad[1, 4:12, 8:72] = pad[1, 4:12, 8:72] + speed[...] * laps[0]
    halo_start(1)
    laps[1] = laplace(1)
    pad[2, 4:12, 8:72] = (
        2.0 * pad[1, 4:12, 8:72] - pad[0, 4:12, 8:72] + wavelet[0, 1] * spot[...]
        + speed[...] * laps[1]
    )
    residual0 = record(pad[1, 4:12, 8:72], 0)
    halo_wait(1)
    close(1, laps.at[1], pad.at[2], speed, True)
    laps[2] = laplace(2)
    third[...] = (
        2.0 * pad[2, 4:12, 8:72] - pad[1, 4:12, 8:72] + wavelet[0, 2] * spot[...]
        + speed[...] * laps[2]
    )
    residual1 = record(pad[2, 4:12, 8:72], 1)
    halo_wait(2)
    close(2, laps.at[2], third, speed, False)
    residual2 = record(third[...], 2)

    field_wait(2)
    adj[0] = after_now[...] + inject(residual2)
    pad[3, 4:12, 8:72] = speed[...] * adj[0]
    halo_start(3)
    field_wait(3)
    adj[1] = 2.0 * adj[0] - after[...] + inject(residual1) + laplace(3)
    pad[4, 4:12, 8:72] = speed[...] * adj[1]
    images[:, 0:64] = adj[0] * laps[2]
    halo_wait(3)
    close(3, adj.at[1], pad.at[4], speed, True)
    third[...] = 2.0 * adj[1] - adj[0] + inject(residual0) + laplace(4)
    images[:, 0:64] = images[:, 0:64] + adj[1] * laps[1] + third[...] * laps[0]
    halo_wait(4)
    close(4, None, images, laps.at[0], False)
    images[:, 64:128] = images[:, 0:64]

    for r in range(8):
        line = images[r, pl.ds(64 - turn, 64)]
        for e in range(2):
            for b in range(2):
                for core in range(2):
                    t = 4 * e + 2 * b + core
                    back_half[b, e, core, r] = line[8 * t : 8 * t + 8]

    def bh_copy(g):
        return push(
            back_half.at[1 - yh, :, :, :, part(g), :], back_in.at[:, :, :, part(g), :],
            bh_send.at[g], bh_recv.at[g], partner,
        )

    for g in range(PARTS):
        bh_copy(g).start()

    def owned(other, g):
        zz, core = other // 2, other % 2
        e, q = zz % 2, zz // 2
        place = 32 * e + 16 * yh + 8 * core + WIDE * g + lax.broadcasted_iota(I32, (WIDE, 128), 0)
        wraps = jnp.where(place < turn, 1, 0)
        mine = (wraps + ((oy >> 6) + yh) == q)[None]
        theirs = (wraps + ((oy >> 6) + 1 - yh) == q)[None]
        return jnp.where(mine, back_half[yh, e, core, :, part(g), :], 0.0) + jnp.where(
            theirs, back_in[e, core, :, part(g), :], 0.0
        )

    def bs_copy(g, d):
        return push(
            back_send.at[d, :, part(g), :],
            back_rows[g].at[pl.ds(pl.multiple_of(8 * k, 8), 8), part(g), :],
            bs_send.at[g, d], bs_recv.at[g, d], at_k((k + d) % 16),
        )

    for g in range(PARTS):
        landed(back_in.at[:, :, :, part(g), :], bh_recv.at[g])

        def give(n, carry):
            d = (n + 8) % 16
            back_send[d, :, part(g), :] = owned((k + d) % 16, g)
            bs_copy(g, d).start()
            return carry

        lax.fori_loop(0, 8, give, 0)
        lax.fori_loop(9, 16, give, 0)
        back_rows[g][pl.ds(pl.multiple_of(8 * k, 8), 8), part(g), :] = owned(k, g)

    def bx_copy(g, d):
        return push(
            back_pick.at[d, :, part(g), :], back_in_x.at[x, :, part(g), :],
            bx_send.at[g, d], bx_recv.at[g, d], at_x((x + d) % 4),
        )

    for g in range(PARTS):

        def given(d, carry):
            landed(
                back_rows[g].at[
                    pl.ds(pl.multiple_of(8 * ((k + 16 - d) % 16), 8), 8), part(g), :
                ],
                bs_recv.at[g, d],
            )
            return carry

        lax.fori_loop(1, 16, given, 0)
        for d in (2, 1, 3, 0):
            other = (x + d) % 4

            def turned(n, carry):
                for r in range(8):
                    i = 8 * n + r
                    back_pick[d, i, part(g), :] = back_rows[g][
                        (32 * other + i + 128 - first) & 127, part(g), :
                    ]
                return carry

            lax.fori_loop(0, 4, turned, 0)
            if d:
                bx_copy(g, d).start()
            else:
                back_in_x[x, :, part(g), :] = back_pick[0, :, part(g), :]

    def by_copy(g, d):
        return push(
            back_sum.at[d, :, part(g), :], back_in_y.at[d, :, part(g), :],
            by_send.at[g, d], by_recv.at[g, d], at_y((yl + d) % 4),
        )

    for g in range(PARTS):
        for d in (1, 3, 2):
            landed(back_in_x.at[(x + 4 - d) % 4, :, part(g), :], bx_recv.at[g, d])
        for d in (2, 1, 3, 0):
            total = jnp.zeros((32, WIDE, 128), F32)
            for other in range(4):
                total += jnp.where(
                    super_of(other, g) == (yl + d) % 4, back_in_x[other, :, part(g), :], 0.0
                )
            back_sum[d, :, part(g), :] = total
            if d:
                by_copy(g, d).start()
    for g in range(PARTS):
        for d in (1, 2, 3):
            landed(back_in_y.at[d, :, part(g), :], by_recv.at[g, d])
    out[...] = back_sum[0] + back_in_y[1] + back_in_y[2] + back_in_y[3]

    for d in (1, 2, 3):
        a_copy(d).wait_send()
    for g in range(PARTS):
        for d in (1, 2, 3):

            @pl.when(y_direct(d))
            def _():
                y_copy(g, d).wait_send()

            x_copy(g, d).wait_send()
            bx_copy(g, d).wait_send()
            by_copy(g, d).wait_send()

        def left(d, carry):
            s_copy(g, d).wait_send()
            bs_copy(g, d).wait_send()
            return carry

        lax.fori_loop(1, 16, left, 0)
        h_copy(g).wait_send()
        bh_copy(g).wait_send()

        @pl.when(inner)
        def _():
            y_relay(g).wait_send()
    for n in range(5):
        halo_done(n)
    for n in range(4):
        for h in range(2):

            @pl.when(jnp.logical_not(stays(h)))
            def _():
                field_copy(n, h).wait_send()


def on_device(
    courant, anchor, source, wavelet, receivers, observed,
    wave_before, wave_now, adjoint_after, adjoint_now,
):
    vmem, smem = pltpu.VMEM, pltpu.SMEM
    dma = pltpu.SemaphoreType.DMA
    return pl.pallas_call(
        kernel,
        out_shape=jax.ShapeDtypeStruct((32, 8, 128), F32),
        in_specs=[pl.BlockSpec(memory_space=pltpu.HBM)] * 10,
        out_specs=pl.BlockSpec(memory_space=vmem),
        scratch_shapes=[
            vmem((4, 32, 8, 128), F32),
            vmem((4, 32, 8, 128), F32),
            vmem((128, 8, 128), F32),
            vmem((128, 8, 128), F32),
            vmem((16, 8, 8, 128), F32),
            vmem((16, 8, 8, 128), F32),
            vmem((16, 8, 8, 128), F32),
            vmem((2, 2, 8, 8, 128), F32),
            vmem((2, 2, 2, 8, 8, 128), F32),
            vmem((8, 128, 128), F32),
            vmem((8, 64, 128), F32),
            vmem((5, 16, 80, 128), F32),
            vmem((5, 2, 4, 64, 128), F32),
            vmem((5, 8, 24, 128), F32),
            vmem((8, 64, 128), F32),
            vmem((8, 64, 128), F32),
            vmem((8, 64, 128), F32),
            vmem((3, 8, 64, 128), F32),
            vmem((8, 64, 128), F32),
            vmem((2, 8, 64, 128), F32),
            vmem((8, 64, 128), F32),
            vmem((8, 128, 128), F32),
            vmem((2, 2, 2, 8, 8, 128), F32),
            vmem((2, 2, 8, 8, 128), F32),
            vmem((16, 8, 8, 128), F32),
            vmem((128, 8, 128), F32),
            vmem((128, 8, 128), F32),
            vmem((4, 32, 8, 128), F32),
            vmem((4, 32, 8, 128), F32),
            vmem((4, 32, 8, 128), F32),
            vmem((4, 32, 8, 128), F32),
            vmem((4, 8, 128), I32),
            vmem((8, 128), I32),
            smem((1, 2), I32),
            smem((1, 3), I32),
            smem((1, 3), F32),
            vmem((3, 1, 64), I32),
            vmem((3, 1, 64), F32),
            vmem((128, 128), F32),
            vmem((64, 512), F32),
            vmem((64, 128), F32),
            vmem((3, 64, 1), F32),
            dma((6,)),
            dma((4, 2)), dma((4, 2)),
            dma((PARTS, 4)), dma((PARTS, 4)),
            dma((4,)), dma((4,)),
            dma((PARTS, 4)), dma((PARTS, 4)),
            dma((PARTS, 16)), dma((PARTS, 16)),
            dma((PARTS,)), dma((PARTS,)),
            dma((5, 3)), dma((5, 3)),
            dma((PARTS,)), dma((PARTS,)),
            dma((PARTS, 16)), dma((PARTS, 16)),
            dma((PARTS, 4)), dma((PARTS, 4)),
            dma((PARTS, 4)), dma((PARTS, 4)),
            dma((PARTS,)),
        ],
        compiler_params=pltpu.CompilerParams(
            collective_id=0, has_side_effects=True, vmem_limit_bytes=60 * 1024 * 1024
        ),
    )(
        anchor, source, wavelet, receivers.transpose(2, 0, 1), observed.transpose(1, 0, 2), courant,
        wave_before, wave_now, adjoint_after, adjoint_now,
    )


def solution(mesh):
    return jax.shard_map(
        on_device,
        mesh=mesh,
        in_specs=(
            P("shot", "space", None),
            P("shot", None),
            P("shot", None),
            P("shot", None),
            P("shot", None, None),
            P("shot", None, None),
            P("shot", "space", None, None),
            P("shot", "space", None, None),
            P("shot", "space", None, None),
            P("shot", "space", None, None),
        ),
        out_specs=P("shot", "space", None),
        check_vma=False,
    )
```
